512 devices in a mesh: grp: 32 (over z_lo, y), rep: 16 (over z_hi, x, core).
Axes of the slice: x: 4, y: 8, z: 8 (z_hi: 2, z_lo: 4; z = z_hi * 4 + z_lo), core: 2. Of those that a mesh axis runs over, the one named last changes fastest.
Arguments:
- embeddings: bfloat16 [98304, 1024], P(('grp', 'rep'))
- labels: int32 [98304], P(('grp', 'rep')), may hold values from 0 to 31, as said below
- order: int32 [98304], P(('grp', 'rep')), may hold values from 0 to 98303, each once
Outputs:
- best: float32 [98304], P(('grp', 'rep'))
The draws below stay inside these ranges and needn't reach their ends.
Inputs may be any that keep to these rules, and one draw needn't show every extreme that they name: `labels`: the indices of grp form consecutive runs of 1 to 4 indices (cluster groups); all members on the devices of one run have one cluster number, and no other run has it; the first run has 4 indices. `order`: each value appears once.
All inputs are finite; a program needn't handle non-finite values.
Results may differ from the reference program's by a relative error of at most 0.00051.
Values may be sent and summed in bfloat16 or wider, within the bound.
No kernel may reach another device: no remote copies, remote signals or barrier semaphores. Data moves between devices by JAX's collectives and lax.ppermute only.
A program may use at most 64 MiB of HBM per device.

```python
import jax
import jax.numpy as jnp
from jax import lax

D = 1024
GMAX = 4
KMAX = 1
PANEL = 3072
MEMBERS = 98304


def layout_rows(key):
    key_size, key_label, key_delta, key_pick = jax.random.split(key, 4)
    count = MEMBERS // PANEL
    run_sizes = jax.random.randint(key_size, (count,), 1, GMAX + 1)
    run_sizes = run_sizes.at[0].set(GMAX)
    run_ends = jnp.cumsum(run_sizes)
    run_starts = run_ends - run_sizes
    grp_positions = jnp.arange(count)
    run_of_grp = jnp.sum((run_ends[None, :] <= grp_positions[:, None]).astype(jnp.int32), axis=1)
    start_of_grp = run_starts[run_of_grp]
    tag_of_grp = jnp.where(run_of_grp == run_of_grp[count - 1], count - 1, start_of_grp)
    positions = jnp.arange(MEMBERS)
    run_of_row = run_of_grp[positions // PANEL]
    tag_of_row = tag_of_grp[positions // PANEL]
    offsets = jax.random.randint(key_label, (MEMBERS,), 0, KMAX)
    offsets = offsets.at[0].set(0).at[MEMBERS - 1].set(KMAX - 1)
    base_label = tag_of_row * KMAX + offsets
    delta = jax.random.randint(key_delta, (MEMBERS,), 1, GMAX * PANEL)
    partner = jnp.maximum(positions - delta, 0)
    copied = (positions - delta >= 0) & (run_of_row[partner] == run_of_row)
    copied = copied & (jax.random.randint(key_pick, (MEMBERS,), 0, 4) == 0)
    copied = copied.at[MEMBERS - 1].set(False)
    final_label = jnp.where(copied, base_label[partner], base_label)
    return (final_label.astype(jnp.int32), partner, copied)


def draw_labels(key, part):
    final_label, partner, copied = layout_rows(key)
    return final_label


def draw_embeddings(key, part):
    final_label, partner, copied = layout_rows(key)
    key = jax.random.fold_in(key, 7)
    key_centre, key_noise, key_copy = jax.random.split(key, 3)
    centres = jax.random.normal(key_centre, (KMAX * (MEMBERS // PANEL), D), jnp.float32)
    noise = jax.random.normal(key_noise, (MEMBERS, D), jnp.float32)
    base_rows = 0.6 * centres[final_label] + noise
    copies = base_rows[partner] + 0.3 * jax.random.normal(key_copy, (MEMBERS, D), jnp.float32)
    values = jnp.where(copied[:, None], copies, base_rows)
    return values.astype(jnp.bfloat16)


def setup_inputs(seed: int = 0) -> dict:
    streams_of = jax.random.split(jax.random.key(seed), 4)
    embeddings = draw_embeddings(jax.random.fold_in(streams_of[3], 71), 0)
    labels = draw_labels(jax.random.fold_in(streams_of[3], 71), 0)
    order = jax.random.permutation(streams_of[2], MEMBERS).astype(jnp.int32)
    return {"embeddings": embeddings, "labels": labels, "order": order}


def reference(embeddings, labels, order):
    values = embeddings.astype(jnp.float32)
    unit = (values * lax.rsqrt(lax.optimization_barrier(jnp.sum(values * values, axis=1, keepdims=True)) + 1e-06)).astype(jnp.bfloat16)
    reach = GMAX - 1
    padded_unit = jnp.pad(unit, ((reach * PANEL, reach * PANEL), (0, 0)))
    padded_label = jnp.pad(labels, (reach * PANEL, reach * PANEL), constant_values=-1)
    padded_order = jnp.pad(order, (reach * PANEL, reach * PANEL))
    count = MEMBERS // PANEL

    def one_panel(index):
        start = (index * PANEL).astype(jnp.int32)
        rows = lax.dynamic_slice_in_dim(unit, start, PANEL, 0)
        row_label = lax.dynamic_slice_in_dim(labels, start, PANEL, 0)
        row_order = lax.dynamic_slice_in_dim(order, start, PANEL, 0)
        window = lax.dynamic_slice_in_dim(padded_unit, start, (2 * reach + 1) * PANEL, 0)
        win_label = lax.dynamic_slice_in_dim(padded_label, start, (2 * reach + 1) * PANEL, 0)
        win_order = lax.dynamic_slice_in_dim(padded_order, start, (2 * reach + 1) * PANEL, 0)
        sims = jnp.dot(rows, window.T, preferred_element_type=jnp.float32)
        mask = (row_label[:, None] == win_label[None, :]) & (win_order[None, :] < row_order[:, None])
        return lax.optimization_barrier(jnp.max(jnp.where(mask, sims, -1.0), axis=1))
    best = lax.map(one_panel, jnp.arange(count, dtype=jnp.int32))
    return best.reshape(MEMBERS)
```

```python
import functools

import jax
import jax.numpy as jnp
from jax import lax
from jax.experimental import pallas as pl
from jax.experimental.pallas import tpu as pltpu
from jax.sharding import Mesh, PartitionSpec as P

ROWS = 192
EXTRA = 16
PACK = ROWS + EXTRA
D = 1024
NEAR = 4
XC = 8
TILE = 256
FAR = 1.0e9


def pack_kernel(emb_ref, lab_ref, ord_ref, out_ref):
    values = emb_ref[...].astype(jnp.float32)
    scale = lax.rsqrt(jnp.sum(values * values, axis=1, keepdims=True) + 1e-06)
    out_ref[0:ROWS, :] = (values * scale).astype(jnp.bfloat16)
    rank = jnp.broadcast_to(ord_ref[...], (EXTRA, ROWS))
    label = jnp.broadcast_to(lab_ref[...], (EXTRA, ROWS))
    line = lax.broadcasted_iota(jnp.int32, (EXTRA, ROWS), 0)
    digits = jnp.where(
        line == 0,
        rank >> 12,
        jnp.where(line == 1, (rank >> 6) & 63, jnp.where(line == 2, rank & 63, label + 1)),
    )
    digits = jnp.where(line < 4, digits, 0).astype(jnp.float32)
    digits = jnp.concatenate([digits, jnp.zeros((EXTRA, D - ROWS), jnp.float32)], axis=1)
    out_ref[ROWS:PACK, :] = digits.astype(jnp.bfloat16)


def pack(embeddings, labels, order):
    return pl.pallas_call(
        pack_kernel,
        out_shape=jax.ShapeDtypeStruct((PACK, D), jnp.bfloat16),
        name="normalize_pack",
        cost_estimate=pl.CostEstimate(flops=4 * ROWS * D, bytes_accessed=4 * ROWS * D, transcendentals=ROWS),
    )(embeddings, labels.reshape(1, ROWS), order.reshape(1, ROWS))


def ranks(extra):
    digits = extra.astype(jnp.float32)
    return digits[0:1, :ROWS] * 4096.0 + digits[1:2, :ROWS] * 64.0 + digits[2:3, :ROWS]


def half_kernel(
    own_ref, a_ref, b_ref, c_ref, panel_ref, prior_ref, cols_ref, rows_ref,
    left, left_extra, right, right_extra, rank_col, row_best, near_sem, panel_sem,
):
    copies = []
    for s, ref in enumerate((own_ref, a_ref, b_ref, c_ref)):
        copies.append(pltpu.make_async_copy(ref.at[ROWS:PACK], left_extra.at[s], near_sem.at[2 * s]))
        copies.append(pltpu.make_async_copy(ref.at[0:ROWS], left.at[s * ROWS:(s + 1) * ROWS], near_sem.at[2 * s + 1]))
    for k in range(XC):
        copies.append(pltpu.make_async_copy(panel_ref.at[k, ROWS:PACK], right_extra.at[k], panel_sem.at[2 * k]))
        copies.append(
            pltpu.make_async_copy(panel_ref.at[k, 0:ROWS], right.at[k * ROWS:(k + 1) * ROWS], panel_sem.at[2 * k + 1])
        )
    for copy in copies:
        copy.start()
    for copy in copies:
        copy.wait()
    own_label = left_extra[0].astype(jnp.float32)[3:4, :ROWS]
    same = [left_extra[s].astype(jnp.float32)[3:4, :ROWS] == own_label for s in range(NEAR)]
    near_rank = jnp.concatenate(
        [jnp.where(same[s], ranks(left_extra[s]), FAR) for s in range(NEAR)], axis=1
    )
    rank_col[...] = jnp.transpose(jnp.broadcast_to(near_rank, (128, NEAR * ROWS)), (1, 0))
    panel_rank = jnp.concatenate([ranks(right_extra[k]) for k in range(XC)], axis=1)
    row_best[...] = jnp.full(row_best.shape, -1.0, jnp.float32)
    cols = []
    for t in range(XC * ROWS // TILE):
        sims = lax.dot_general(
            left[...], right[t * TILE:(t + 1) * TILE, :], (((1,), (1,)), ((), ())),
            preferred_element_type=jnp.float32,
        )
        for h in range(TILE // 128):
            part = sims[:, h * 128:(h + 1) * 128]
            rank_row = panel_rank[:, t * TILE + h * 128:t * TILE + (h + 1) * 128]
            here = part[:ROWS]
            best = jnp.max(jnp.where(rank_col[:ROWS] < rank_row, here, -1.0), axis=0, keepdims=True)
            there = part[ROWS:]
            earlier = rank_row < rank_col[ROWS:]
            best = jnp.maximum(best, jnp.max(jnp.where(earlier, -1.0, there), axis=0, keepdims=True))
            row_best[...] = jnp.maximum(row_best[...], jnp.where(earlier, there, -1.0))
            cols.append(best)
    best = jnp.concatenate(cols, axis=1)
    for k in range(XC):
        cols_ref[k:k + 1, :] = best[:, k * ROWS:(k + 1) * ROWS]
    rows = jnp.max(jnp.transpose(row_best[...], (1, 0)), axis=0, keepdims=True)
    for s in range(1, NEAR):
        line = jnp.where(same[s], rows[:, (s - 1) * ROWS:s * ROWS], -1.0)
        rows_ref[s - 1] = jnp.maximum(line, prior_ref[s - 1])


def half(own, near, panel, prior):
    anywhere = pl.BlockSpec(memory_space=pl.ANY)
    inside = pl.BlockSpec(memory_space=pltpu.VMEM)
    return pl.pallas_call(
        half_kernel,
        out_shape=(
            jax.ShapeDtypeStruct((XC, ROWS), jnp.float32),
            jax.ShapeDtypeStruct((NEAR - 1, 1, ROWS), jnp.float32),
        ),
        in_specs=[anywhere] * 5 + [inside],
        out_specs=(inside, inside),
        scratch_shapes=[
            pltpu.VMEM((NEAR * ROWS, D), jnp.bfloat16),
            pltpu.VMEM((NEAR, EXTRA, D), jnp.bfloat16),
            pltpu.VMEM((XC * ROWS, D), jnp.bfloat16),
            pltpu.VMEM((XC, EXTRA, D), jnp.bfloat16),
            pltpu.VMEM((NEAR * ROWS, 128), jnp.float32),
            pltpu.VMEM(((NEAR - 1) * ROWS, 128), jnp.float32),
            pltpu.SemaphoreType.DMA((2 * NEAR,)),
            pltpu.SemaphoreType.DMA((2 * XC,)),
        ],
        compiler_params=pltpu.CompilerParams(vmem_limit_bytes=40 * 1024 * 1024),
        name="half_maxima",
        cost_estimate=pl.CostEstimate(
            flops=2 * NEAR * XC * ROWS * ROWS * D, bytes_accessed=2 * (NEAR + XC) * PACK * D, transcendentals=0
        ),
    )(own, *near, panel, prior)


def shift(value, steps, count):
    pairs = [(i, i + steps) for i in range(count) if 0 <= i + steps < count]
    return lax.ppermute(value, "grp", pairs)


def per_device(embeddings, labels, order):
    count = lax.axis_size("grp")
    grp = lax.axis_index("grp")
    zh = lax.axis_index("zh")
    block = pack(embeddings, labels, order)
    flipped = lax.ppermute(block, "zh", [(0, 1), (1, 0)])
    panel = lax.all_gather(block, "xc", axis=0, tiled=False)
    moves = (3 * -1, 1, 2)
    near = [shift(block, steps, count) for steps in moves]
    other = lax.all_gather(flipped, "xc", axis=0, tiled=False)
    prior = jnp.full((NEAR - 1, 1, ROWS), -1.0, jnp.float32)
    cols_own, prior = half(block, near, panel, prior)
    cols_other, rows = half(block, near, other, prior)
    cols = jnp.where(
        zh == 0,
        jnp.concatenate([cols_own, cols_other], axis=0),
        jnp.concatenate([cols_other, cols_own], axis=0),
    )
    best = jnp.max(lax.all_to_all(cols, ("zh", "xc"), 0, 0, tiled=True), axis=0)
    for i, steps in enumerate(moves):
        back = shift(rows[i], -steps, count).reshape(ROWS)
        source = grp + steps
        best = jnp.maximum(best, jnp.where((source >= 0) & (source < count), back, -1.0))
    return best


def solution(mesh):
    fine = Mesh(mesh.devices.reshape(mesh.shape["grp"], 2, XC), ("grp", "zh", "xc"))
    spec = P(("grp", "zh", "xc"))
    return jax.shard_map(
        per_device,
        mesh=fine,
        in_specs=(P(("grp", "zh", "xc"), None), spec, spec),
        out_specs=spec,
        check_vma=False,
    )
```

```python
import jax
import jax.numpy as jnp
from jax import lax
from jax.experimental import pallas as pl
from jax.experimental.pallas import tpu as pltpu
from jax.sharding import Mesh, PartitionSpec as P

ROWS = 192
EXTRA = 16
PACK = ROWS + EXTRA
D = 1024
X = 4
MOVES = (-3, 1, 2)
NEAR = 1 + len(MOVES)
LEFT = 2 * NEAR * ROWS
TILE = 256
FAR = 1.0e9


def pack_kernel(emb_ref, lab_ref, ord_ref, out_ref):
    values = emb_ref[...].astype(jnp.float32)
    scale = lax.rsqrt(jnp.sum(values * values, axis=1, keepdims=True) + 1e-06)
    out_ref[0:ROWS, :] = (values * scale).astype(jnp.bfloat16)
    rank = jnp.broadcast_to(ord_ref[...], (EXTRA, ROWS))
    label = jnp.broadcast_to(lab_ref[...], (EXTRA, ROWS))
    line = lax.broadcasted_iota(jnp.int32, (EXTRA, ROWS), 0)
    digits = jnp.where(
        line == 0,
        rank >> 12,
        jnp.where(line == 1, (rank >> 6) & 63, jnp.where(line == 2, rank & 63, label + 1)),
    )
    digits = jnp.where(line < 4, digits, 0).astype(jnp.float32)
    digits = jnp.concatenate([digits, jnp.zeros((EXTRA, D - ROWS), jnp.float32)], axis=1)
    out_ref[ROWS:PACK, :] = digits.astype(jnp.bfloat16)


def pack(embeddings, labels, order):
    return pl.pallas_call(
        pack_kernel,
        out_shape=jax.ShapeDtypeStruct((PACK, D), jnp.bfloat16),
        name="normalize_pack",
        cost_estimate=pl.CostEstimate(flops=4 * ROWS * D, bytes_accessed=4 * ROWS * D, transcendentals=ROWS),
    )(embeddings, labels.reshape(1, ROWS), order.reshape(1, ROWS))


def ranks(extra):
    return extra[0:1] * 4096.0 + extra[1:2] * 64.0 + extra[2:3]


def extra_of(ref):
    return ref[ROWS:PACK, 0:256].astype(jnp.float32)[:, :ROWS]


def half_kernel(place_ref, *refs):
    near = refs[:2 * NEAR]
    panel = refs[2 * NEAR:2 * NEAR + X]
    prior_ref, cols_ref, rows_ref, left, right, rank_col, row_best = refs[2 * NEAR + X:]
    for s in range(2 * NEAR):
        left[s * ROWS:(s + 1) * ROWS, :] = near[s][0:ROWS, :]
    for k in range(X):
        right[k * ROWS:(k + 1) * ROWS, :] = panel[k][0:ROWS, :]
    extras = [extra_of(ref) for ref in near]
    same = [extra[3:4] == extras[0][3:4] for extra in extras]
    near_rank = jnp.concatenate(
        [jnp.where(same[s], ranks(extras[s]), FAR) for s in range(2 * NEAR)], axis=1
    )
    rank_col[...] = jnp.transpose(jnp.broadcast_to(near_rank, (128, LEFT)), (1, 0))
    panel_rank = jnp.concatenate([ranks(extra_of(ref)) for ref in panel], axis=1)
    row_best[...] = jnp.full(row_best.shape, -1.0, jnp.float32)
    cols = []
    split = 2 * ROWS
    for t in range(X * ROWS // TILE):
        sims = lax.dot_general(
            left[...], right[t * TILE:(t + 1) * TILE, :], (((1,), (1,)), ((), ())),
            preferred_element_type=jnp.float32,
        )
        for h in range(TILE // 128):
            part = sims[:, h * 128:(h + 1) * 128]
            rank_row = panel_rank[:, t * TILE + h * 128:t * TILE + (h + 1) * 128]
            here = part[:split]
            best = jnp.max(jnp.where(rank_col[:split] < rank_row, here, -1.0), axis=0, keepdims=True)
            there = part[split:]
            earlier = rank_row < rank_col[split:]
            best = jnp.maximum(best, jnp.max(jnp.where(earlier, -1.0, there), axis=0, keepdims=True))
            row_best[...] = jnp.maximum(row_best[...], jnp.where(earlier, there, -1.0))
            cols.append(best)
    best = jnp.concatenate(cols, axis=1)
    for k in range(X):
        cols_ref[place_ref[k]] = best[:, k * ROWS:(k + 1) * ROWS]
    rows = jnp.max(jnp.transpose(row_best[...], (1, 0)), axis=0, keepdims=True)
    for s in range(2, 2 * NEAR):
        line = jnp.where(same[s], rows[:, (s - 2) * ROWS:(s - 1) * ROWS], -1.0)
        rows_ref[s - 2] = jnp.maximum(line, prior_ref[s - 2])


def half(place, near, panel, prior):
    inside = pl.BlockSpec(memory_space=pltpu.VMEM)
    return pl.pallas_call(
        half_kernel,
        out_shape=(
            jax.ShapeDtypeStruct((X, 1, ROWS), jnp.float32),
            jax.ShapeDtypeStruct((2 * (NEAR - 1), 1, ROWS), jnp.float32),
        ),
        in_specs=[pl.BlockSpec(memory_space=pltpu.SMEM)] + [inside] * (2 * NEAR + X + 1),
        out_specs=(inside, inside),
        scratch_shapes=[
            pltpu.VMEM((LEFT, D), jnp.bfloat16),
            pltpu.VMEM((X * ROWS, D), jnp.bfloat16),
            pltpu.VMEM((LEFT, 128), jnp.float32),
            pltpu.VMEM((LEFT - 2 * ROWS, 128), jnp.float32),
        ],
        compiler_params=pltpu.CompilerParams(vmem_limit_bytes=40 * 1024 * 1024),
        name="half_maxima",
        cost_estimate=pl.CostEstimate(
            flops=2 * LEFT * X * ROWS * D, bytes_accessed=2 * (2 * NEAR + X) * PACK * D, transcendentals=0
        ),
    )(place, *near, *panel, prior)


def shift(value, steps, count):
    pairs = [(i, i + steps) for i in range(count) if 0 <= i + steps < count]
    return lax.ppermute(value, "grp", pairs)


def swap(value, axis):
    return lax.ppermute(value, axis, [(0, 1), (1, 0)])


def spread(block, core):
    ahead = lax.ppermute(block, "x", [(i, (i + 1) % X) for i in range(X)])
    behind = lax.ppermute(block, "x", [(i, (i + X - 1) % X) for i in range(X)])
    pairs = [(2 * i, 2 * ((i + 1) % X)) for i in range(X)]
    pairs += [(2 * i + 1, 2 * ((i + X - 1) % X) + 1) for i in range(X)]
    across = lax.ppermute(jnp.where(core == 0, ahead, behind), ("x", "core"), pairs)
    return [block, ahead, behind, across]


def per_device(embeddings, labels, order):
    count = lax.axis_size("grp")
    grp, zh, x, core = (lax.axis_index(axis) for axis in ("grp", "zh", "x", "core"))
    block = pack(embeddings, labels, order)
    flipped = swap(block, "zh")
    near = [block] + [shift(block, steps, count) for steps in MOVES]
    panel = spread(block, core)
    other = spread(flipped, core)
    both = []
    for value in near:
        both += [value, swap(value, "core")]
    place = jnp.stack([x, (x + X - 1) % X, (x + 1) % X, (x + 2) % X]).astype(jnp.int32)
    prior = jnp.full((2 * (NEAR - 1), 1, ROWS), -1.0, jnp.float32)
    cols_own, prior = half(place, both, panel, prior)
    cols_other, rows = half(place, both, other, prior)
    cols = jnp.where(
        zh == 0,
        jnp.concatenate([cols_own, cols_other], axis=0),
        jnp.concatenate([cols_other, cols_own], axis=0),
    )
    best = jnp.max(lax.all_to_all(cols, ("zh", "x"), 0, 0, tiled=True), axis=0)
    mine = jnp.maximum(rows[0::2], swap(rows[1::2], "core"))
    for i, steps in enumerate(MOVES):
        back = shift(mine[i], -steps, count)
        source = grp + steps
        best = jnp.maximum(best, jnp.where((source >= 0) & (source < count), back, -1.0))
    return best.reshape(ROWS)


def solution(mesh):
    axes = ("grp", "zh", "x", "core")
    fine = Mesh(mesh.devices.reshape(mesh.shape["grp"], 2, X, 2), axes)
    return jax.shard_map(
        per_device,
        mesh=fine,
        in_specs=(P(axes, None), P(axes), P(axes)),
        out_specs=P(axes),
        check_vma=False,
    )
```

```python
import jax
import jax.numpy as jnp
from jax import lax
from jax.experimental import pallas as pl
from jax.experimental.pallas import tpu as pltpu
from jax.sharding import Mesh, PartitionSpec as P

ROWS = 192
EXTRA = 16
PACK = ROWS + EXTRA
D = 1024
X = 4
MOVES = (-3, 1, 2)
NEAR = 1 + len(MOVES)
LEFT = 2 * NEAR * ROWS
TILE = 256
FAR = 1.0e9


def pack_kernel(emb_ref, lab_ref, ord_ref, out_ref):
    values = emb_ref[...].astype(jnp.float32)
    scale = lax.rsqrt(jnp.sum(values * values, axis=1, keepdims=True) + 1e-06)
    out_ref[0:ROWS, :] = (values * scale).astype(jnp.bfloat16)
    rank = jnp.broadcast_to(ord_ref[...], (EXTRA, ROWS))
    label = jnp.broadcast_to(lab_ref[...], (EXTRA, ROWS))
    line = lax.broadcasted_iota(jnp.int32, (EXTRA, ROWS), 0)
    digits = jnp.where(
        line == 0,
        rank >> 12,
        jnp.where(line == 1, (rank >> 6) & 63, jnp.where(line == 2, rank & 63, label + 1)),
    )
    digits = jnp.where(line < 4, digits, 0).astype(jnp.float32)
    digits = jnp.concatenate([digits, jnp.zeros((EXTRA, D - ROWS), jnp.float32)], axis=1)
    out_ref[ROWS:PACK, :] = digits.astype(jnp.bfloat16)


def pack(embeddings, labels, order):
    return pl.pallas_call(
        pack_kernel,
        out_shape=jax.ShapeDtypeStruct((PACK, D), jnp.bfloat16),
        name="normalize_pack",
        cost_estimate=pl.CostEstimate(flops=4 * ROWS * D, bytes_accessed=4 * ROWS * D, transcendentals=ROWS),
    )(embeddings, labels.reshape(1, ROWS), order.reshape(1, ROWS))


def ranks(extra):
    return extra[0:1] * 4096.0 + extra[1:2] * 64.0 + extra[2:3]


def extra_of(ref):
    return ref[ROWS:PACK, 0:256].astype(jnp.float32)[:, :ROWS]


def repeat_kernel(block_ref, out_ref):
    for k in range(X):
        out_ref[k] = block_ref[...]


def repeat(block):
    return pl.pallas_call(
        repeat_kernel,
        out_shape=jax.ShapeDtypeStruct((X, PACK, D), jnp.bfloat16),
        name="repeat",
        cost_estimate=pl.CostEstimate(flops=0, bytes_accessed=2 * (X + 1) * PACK * D, transcendentals=0),
    )(block)


def half_kernel(*refs):
    near = refs[:2 * NEAR]
    panel_ref, prior_ref, cols_ref, rows_ref, left, right, rank_col, row_best = refs[2 * NEAR:]
    panel = [panel_ref.at[k] for k in range(X)]
    for s in range(2 * NEAR):
        left[s * ROWS:(s + 1) * ROWS, :] = near[s][0:ROWS, :]
    for k in range(X):
        right[k * ROWS:(k + 1) * ROWS, :] = panel[k][0:ROWS, :]
    extras = [extra_of(ref) for ref in near]
    same = [extra[3:4] == extras[0][3:4] for extra in extras]
    near_rank = jnp.concatenate(
        [jnp.where(same[s], ranks(extras[s]), FAR) for s in range(2 * NEAR)], axis=1
    )
    rank_col[...] = jnp.transpose(jnp.broadcast_to(near_rank, (128, LEFT)), (1, 0))
    panel_rank = jnp.concatenate([ranks(extra_of(ref)) for ref in panel], axis=1)
    row_best[...] = jnp.full(row_best.shape, -1.0, jnp.float32)
    cols = []
    split = 2 * ROWS
    for t in range(X * ROWS // TILE):
        sims = lax.dot_general(
            left[...], right[t * TILE:(t + 1) * TILE, :], (((1,), (1,)), ((), ())),
            preferred_element_type=jnp.float32,
        )
        for h in range(TILE // 128):
            part = sims[:, h * 128:(h + 1) * 128]
            rank_row = panel_rank[:, t * TILE + h * 128:t * TILE + (h + 1) * 128]
            here = part[:split]
            best = jnp.max(jnp.where(rank_col[:split] < rank_row, here, -1.0), axis=0, keepdims=True)
            there = part[split:]
            earlier = rank_row < rank_col[split:]
            best = jnp.maximum(best, jnp.max(jnp.where(earlier, -1.0, there), axis=0, keepdims=True))
            row_best[...] = jnp.maximum(row_best[...], jnp.where(earlier, there, -1.0))
            cols.append(best)
    best = jnp.concatenate(cols, axis=1)
    for k in range(X):
        cols_ref[k] = best[:, k * ROWS:(k + 1) * ROWS]
    rows = jnp.max(jnp.transpose(row_best[...], (1, 0)), axis=0, keepdims=True)
    for s in range(2, 2 * NEAR):
        line = jnp.where(same[s], rows[:, (s - 2) * ROWS:(s - 1) * ROWS], -1.0)
        rows_ref[s - 2] = jnp.maximum(line, prior_ref[s - 2])


def half(near, panel, prior):
    inside = pl.BlockSpec(memory_space=pltpu.VMEM)
    return pl.pallas_call(
        half_kernel,
        out_shape=(
            jax.ShapeDtypeStruct((X, 1, ROWS), jnp.float32),
            jax.ShapeDtypeStruct((2 * (NEAR - 1), 1, ROWS), jnp.float32),
        ),
        in_specs=[inside] * (2 * NEAR + 2),
        out_specs=(inside, inside),
        scratch_shapes=[
            pltpu.VMEM((LEFT, D), jnp.bfloat16),
            pltpu.VMEM((X * ROWS, D), jnp.bfloat16),
            pltpu.VMEM((LEFT, 128), jnp.float32),
            pltpu.VMEM((LEFT - 2 * ROWS, 128), jnp.float32),
        ],
        compiler_params=pltpu.CompilerParams(vmem_limit_bytes=40 * 1024 * 1024),
        name="half_maxima",
        cost_estimate=pl.CostEstimate(
            flops=2 * LEFT * X * ROWS * D, bytes_accessed=2 * (2 * NEAR + X) * PACK * D, transcendentals=0
        ),
    )(*near, panel, prior)


def shift(value, steps, count):
    pairs = [(i, i + steps) for i in range(count) if 0 <= i + steps < count]
    return lax.ppermute(value, "grp", pairs)


def swap(value, axis):
    return lax.ppermute(value, axis, [(0, 1), (1, 0)])


def spread(block):
    return lax.all_to_all(repeat(block), "x", 0, 0, tiled=True)


def per_device(embeddings, labels, order):
    count = lax.axis_size("grp")
    grp, zh = lax.axis_index("grp"), lax.axis_index("zh")
    block = pack(embeddings, labels, order)
    flipped = swap(block, "zh")
    near = [block] + [shift(block, steps, count) for steps in MOVES]
    panel = spread(block)
    other = spread(flipped)
    both = []
    for value in near:
        both += [value, swap(value, "core")]
    prior = jnp.full((2 * (NEAR - 1), 1, ROWS), -1.0, jnp.float32)
    cols_own, prior = half(both, panel, prior)
    cols_other, rows = half(both, other, prior)
    cols = jnp.where(
        zh == 0,
        jnp.concatenate([cols_own, cols_other], axis=0),
        jnp.concatenate([cols_other, cols_own], axis=0),
    )
    best = jnp.max(lax.all_to_all(cols, ("zh", "x"), 0, 0, tiled=True), axis=0)
    mine = jnp.maximum(rows[0::2], swap(rows[1::2], "core"))
    for i, steps in enumerate(MOVES):
        back = shift(mine[i], -steps, count)
        source = grp + steps
        best = jnp.maximum(best, jnp.where((source >= 0) & (source < count), back, -1.0))
    return best.reshape(ROWS)


def solution(mesh):
    axes = ("grp", "zh", "x", "core")
    fine = Mesh(mesh.devices.reshape(mesh.shape["grp"], 2, X, 2), axes)
    return jax.shard_map(
        per_device,
        mesh=fine,
        in_specs=(P(axes, None), P(axes), P(axes)),
        out_specs=P(axes),
        check_vma=False,
    )
```

```python
import jax
import jax.numpy as jnp
from jax import lax
from jax.experimental import pallas as pl
from jax.experimental.pallas import tpu as pltpu
from jax.sharding import Mesh, PartitionSpec as P

ROWS = 192
EXTRA = 16
PACK = ROWS + EXTRA
D = 1024
X = 4
MOVES = (1, -3, 2)
NEAR = 1 + len(MOVES)
LEFT = 2 * NEAR * ROWS
TILE = 256
FAR = 1.0e9


def pack_kernel(emb_ref, lab_ref, ord_ref, out_ref):
    values = emb_ref[...].astype(jnp.float32)
    scale = lax.rsqrt(jnp.sum(values * values, axis=1, keepdims=True) + 1e-06)
    out_ref[0:ROWS, :] = (values * scale).astype(jnp.bfloat16)
    rank = jnp.broadcast_to(ord_ref[...], (EXTRA, ROWS))
    label = jnp.broadcast_to(lab_ref[...], (EXTRA, ROWS))
    line = lax.broadcasted_iota(jnp.int32, (EXTRA, ROWS), 0)
    digits = jnp.where(
        line == 0,
        rank >> 12,
        jnp.where(line == 1, (rank >> 6) & 63, jnp.where(line == 2, rank & 63, label + 1)),
    )
    digits = jnp.where(line < 4, digits, 0).astype(jnp.float32)
    digits = jnp.concatenate([digits, jnp.zeros((EXTRA, D - ROWS), jnp.float32)], axis=1)
    out_ref[ROWS:PACK, :] = digits.astype(jnp.bfloat16)


def pack(embeddings, labels, order):
    return pl.pallas_call(
        pack_kernel,
        out_shape=jax.ShapeDtypeStruct((PACK, D), jnp.bfloat16),
        compiler_params=pltpu.CompilerParams(vmem_limit_bytes=8 * 1024 * 1024),
        name="normalize_pack",
        cost_estimate=pl.CostEstimate(flops=4 * ROWS * D, bytes_accessed=4 * ROWS * D, transcendentals=ROWS),
    )(embeddings, labels.reshape(1, ROWS), order.reshape(1, ROWS))


def ranks(extra):
    return extra[0:1] * 4096.0 + extra[1:2] * 64.0 + extra[2:3]


def pair_kernel(core_ref, block_ref, sib_ref, out_ref):
    core = core_ref[0]
    out_ref[core] = block_ref[...]
    out_ref[1 - core] = sib_ref[...]


def pair(core, block, sib):
    inside = pl.BlockSpec(memory_space=pltpu.VMEM)
    return pl.pallas_call(
        pair_kernel,
        out_shape=jax.ShapeDtypeStruct((2, PACK, D), jnp.bfloat16),
        in_specs=[pl.BlockSpec(memory_space=pltpu.SMEM), inside, inside],
        out_specs=inside,
        compiler_params=pltpu.CompilerParams(vmem_limit_bytes=8 * 1024 * 1024),
        name="pair",
        cost_estimate=pl.CostEstimate(flops=0, bytes_accessed=8 * PACK * D, transcendentals=0),
    )(jnp.reshape(core, (1,)).astype(jnp.int32), block, sib)


def fetch(sources, rows_ref, extra_ref, sems):
    copies = []
    for k, ref in enumerate(sources):
        copies.append(pltpu.make_async_copy(ref.at[ROWS:PACK], extra_ref.at[k], sems.at[2 * k]))
        copies.append(
            pltpu.make_async_copy(ref.at[0:ROWS], rows_ref.at[k * ROWS:(k + 1) * ROWS], sems.at[2 * k + 1])
        )
    for copy in copies:
        copy.start()
    for copy in copies:
        copy.wait()


def extra_of(extra):
    return extra[:, 0:256].astype(jnp.float32)[:, :ROWS]


def prep_kernel(block_ref, sib_ref, first_ref, second_ref, two_ref, two_sib_ref, left_ref, rank_ref, valid_ref, extra_ref, sems):
    near = [block_ref, sib_ref, first_ref.at[0], first_ref.at[1], second_ref.at[0], second_ref.at[1], two_ref, two_sib_ref]
    fetch(near, left_ref, extra_ref, sems)
    extras = [extra_of(extra_ref[s]) for s in range(2 * NEAR)]
    same = [extra[3:4] == extras[0][3:4] for extra in extras]
    near_rank = jnp.concatenate([jnp.where(same[s], ranks(extras[s]), FAR) for s in range(2 * NEAR)], axis=1)
    rank_ref[...] = jnp.transpose(jnp.broadcast_to(near_rank, (128, LEFT)), (1, 0))
    for s in range(2, 2 * NEAR):
        valid_ref[s - 2] = same[s].astype(jnp.float32)


def prep(near):
    inside = pl.BlockSpec(memory_space=pltpu.VMEM)
    return pl.pallas_call(
        prep_kernel,
        out_shape=(
            jax.ShapeDtypeStruct((LEFT, D), jnp.bfloat16),
            jax.ShapeDtypeStruct((LEFT, 128), jnp.float32),
            jax.ShapeDtypeStruct((LEFT // ROWS - 2, 1, ROWS), jnp.float32),
        ),
        in_specs=[pl.BlockSpec(memory_space=pl.ANY)] * len(near),
        out_specs=(inside, inside, inside),
        scratch_shapes=[
            pltpu.VMEM((2 * NEAR, EXTRA, D), jnp.bfloat16),
            pltpu.SemaphoreType.DMA((4 * NEAR,)),
        ],
        compiler_params=pltpu.CompilerParams(vmem_limit_bytes=8 * 1024 * 1024),
        name="near_prep",
        cost_estimate=pl.CostEstimate(flops=0, bytes_accessed=4 * LEFT * D, transcendentals=0),
    )(*near)


def maxima_kernel(blocks, at, first, last, place_ref, left_ref, rank_ref, valid_ref, *refs):
    panel = refs[:blocks]
    *refs, right, extra_ref, sems = refs[blocks:]
    if first:
        cols_ref, *rows_ref = refs
    else:
        prior_cols_ref, prior_ref, cols_ref, *rows_ref = refs
        cols_ref[...] = prior_cols_ref[...]
    width = blocks * ROWS
    fetch(panel, right, extra_ref, sems)
    panel_rank = jnp.concatenate([ranks(extra_of(extra_ref[k])) for k in range(blocks)], axis=1)
    split = 2 * ROWS
    cols = []
    rows = None
    for start in range(0, width, TILE):
        tile = min(TILE, width - start)
        sims = lax.dot_general(
            left_ref[...], right[start:start + tile, :], (((1,), (1,)), ((), ())),
            preferred_element_type=jnp.float32,
        )
        for lane in range(0, tile, 128):
            lanes = min(128, tile - lane)
            part = sims[:, lane:lane + lanes]
            rank_row = panel_rank[:, start + lane:start + lane + lanes]
            rank_col = rank_ref[:, :lanes]
            here = part[:split]
            best = jnp.max(jnp.where(rank_col[:split] < rank_row, here, -1.0), axis=0, keepdims=True)
            there = part[split:]
            earlier = rank_row < rank_col[split:]
            best = jnp.maximum(best, jnp.max(jnp.where(earlier, -1.0, there), axis=0, keepdims=True))
            cols.append(best)
            found = jnp.where(earlier, there, -1.0)
            if lanes < 128:
                found = jnp.concatenate([found, jnp.full((LEFT - split, 128 - lanes), -1.0, jnp.float32)], axis=1)
            rows = found if rows is None else jnp.maximum(rows, found)
    best = jnp.concatenate(cols, axis=1)
    for k in range(blocks):
        cols_ref[place_ref[at + k]] = best[:, k * ROWS:(k + 1) * ROWS]
    if not first:
        rows = jnp.maximum(rows, prior_ref[...])
    if not last:
        rows_ref[0][...] = rows
    else:
        line = jnp.max(jnp.transpose(rows, (1, 0)), axis=0, keepdims=True)
        kept = [
            jnp.where(valid_ref[s] > 0.5, line[:, s * ROWS:(s + 1) * ROWS], -1.0) for s in range(LEFT // ROWS - 2)
        ]
        even = place_ref[2 * X] == 0
        rows_ref[0][0] = jnp.where(even, kept[0], kept[3])
        rows_ref[1][0] = jnp.where(even, kept[1], kept[2])
        rows_ref[0][1] = jnp.where(even, kept[2], kept[1])
        rows_ref[1][1] = jnp.where(even, kept[3], kept[0])
        rows_ref[0][2] = kept[4]
        rows_ref[1][2] = kept[5]


def maxima(place, laid, panel, at, prior, last):
    inside = pl.BlockSpec(memory_space=pltpu.VMEM)
    blocks = len(panel)
    operands = (*laid, *panel, *prior)
    lines = jax.ShapeDtypeStruct((NEAR - 1, 1, ROWS), jnp.float32)
    held = jax.ShapeDtypeStruct((LEFT - 2 * ROWS, 128), jnp.float32)
    rows = (lines, lines) if last else (held,)
    return pl.pallas_call(
        lambda *refs: maxima_kernel(blocks, at, not prior, last, *refs),
        out_shape=(jax.ShapeDtypeStruct((2 * X, 1, ROWS), jnp.float32), *rows),
        in_specs=(
            [pl.BlockSpec(memory_space=pltpu.SMEM)] + [inside] * len(laid)
            + [pl.BlockSpec(memory_space=pl.ANY)] * blocks + [inside] * len(prior)
        ),
        out_specs=(inside,) * (1 + len(rows)),
        scratch_shapes=[
            pltpu.VMEM((blocks * ROWS, D), jnp.bfloat16),
            pltpu.VMEM((blocks, EXTRA, D), jnp.bfloat16),
            pltpu.SemaphoreType.DMA((2 * blocks,)),
        ],
        compiler_params=pltpu.CompilerParams(vmem_limit_bytes=16 * 1024 * 1024),
        name="panel_maxima",
        cost_estimate=pl.CostEstimate(
            flops=2 * LEFT * blocks * ROWS * D, bytes_accessed=2 * (2 * NEAR + blocks) * PACK * D, transcendentals=0
        ),
    )(place, *operands)


def shift(value, steps, count):
    pairs = [(i, i + steps) for i in range(count) if 0 <= i + steps < count]
    return lax.ppermute(value, "grp", pairs)


def swap(value, axis):
    return lax.ppermute(value, axis, [(0, 1), (1, 0)])


def forward(value):
    pairs = [(2 * i, 2 * ((i + 1) % X)) for i in range(X)]
    pairs += [(2 * i + 1, 2 * ((i + X - 1) % X) + 1) for i in range(X)]
    return lax.ppermute(value, ("x", "core"), pairs)


def shift_both(value, even, odd, count):
    pairs = [(2 * i, 2 * (i + even)) for i in range(count) if 0 <= i + even < count]
    pairs += [(2 * i + 1, 2 * (i + odd) + 1) for i in range(count) if 0 <= i + odd < count]
    return lax.ppermute(value, ("grp", "core"), pairs)


def per_device(embeddings, labels, order):
    count = lax.axis_size("grp")
    grp, zh, x, core = (lax.axis_index(axis) for axis in ("grp", "zh", "x", "core"))
    block = pack(embeddings, labels, order)
    sib = swap(block, "core")
    panel = [block, forward(block)]
    both = pair(core, block, sib)
    ready, both = lax.optimization_barrier((block, both))
    first = shift_both(both, MOVES[0], MOVES[1], count)
    flipped = swap(ready, "zh")
    two = shift(ready, MOVES[2], count)
    panel.append(forward(panel[-1]))
    first, flipped, two, panel[-1] = lax.optimization_barrier((first, flipped, two, panel[-1]))
    panel.append(forward(panel[-1]))
    other = [flipped]
    for _ in range(X - 1):
        other.append(forward(other[-1]))
    laid = prep((block, sib, first, swap(first, "core"), two, swap(two, "core")))
    turn = jnp.where(core == 0, 1, X - 1)
    place = [(zh + h) % 2 * X + (x + (X - k) * turn) % X for h in range(2) for k in range(X)]
    place = jnp.stack([*place, core]).astype(jnp.int32)
    cols, rows = maxima(place, laid, panel, 0, (), False)
    cols, rows = maxima(place, laid, other[:3], X, (cols, rows), False)
    cols, rows, rows_sib = maxima(place, laid, other[3:], X + 3, (cols, rows), True)
    best = jnp.max(lax.all_to_all(cols, ("zh", "x"), 0, 0, tiled=True), axis=0)
    mine = jnp.maximum(rows, swap(rows_sib, "core"))
    for i, steps in enumerate(MOVES):
        back = shift(mine[i], -steps, count)
        source = grp + steps
        best = jnp.maximum(best, jnp.where((source >= 0) & (source < count), back, -1.0))
    return best.reshape(ROWS)


def solution(mesh):
    axes = ("grp", "zh", "x", "core")
    fine = Mesh(mesh.devices.reshape(mesh.shape["grp"], 2, X, 2), axes)
    return jax.shard_map(
        per_device,
        mesh=fine,
        in_specs=(P(axes, None), P(axes), P(axes)),
        out_specs=P(axes),
        check_vma=False,
    )
```

```python
import jax
import jax.numpy as jnp
from jax import lax
from jax.experimental import pallas as pl
from jax.experimental.pallas import tpu as pltpu
from jax.sharding import Mesh, PartitionSpec as P

ROWS = 192
EXTRA = 16
PACK = ROWS + EXTRA
D = 1024
X = 4
Z_LO = 4
MOVES = (1, -3, 2)
NEAR = 1 + len(MOVES)
LEFT = 2 * NEAR * ROWS
TILE = 256
FAR = 1.0e9
SLOTS = (0, 7, 1, 2, 3, 4, 5, 6)


def pack_kernel(emb_any, lab_any, ord_any, out_ref, emb_ref, lab_ref, ord_ref, sems):
    copies = [
        pltpu.make_async_copy(source, target, sems.at[k])
        for k, (source, target) in enumerate(((emb_any, emb_ref), (lab_any, lab_ref), (ord_any, ord_ref)))
    ]
    for copy in copies:
        copy.start()
    for copy in copies:
        copy.wait()
    values = emb_ref[...].astype(jnp.float32)
    scale = lax.rsqrt(jnp.sum(values * values, axis=1, keepdims=True) + 1e-06)
    out_ref[0:ROWS, :] = (values * scale).astype(jnp.bfloat16)
    rank = jnp.broadcast_to(ord_ref[...], (EXTRA, ROWS))
    label = jnp.broadcast_to(lab_ref[...], (EXTRA, ROWS))
    line = lax.broadcasted_iota(jnp.int32, (EXTRA, ROWS), 0)
    digits = jnp.where(
        line == 0,
        rank >> 12,
        jnp.where(line == 1, (rank >> 6) & 63, jnp.where(line == 2, rank & 63, label + 1)),
    )
    digits = jnp.where(line < 4, digits, 0).astype(jnp.float32)
    digits = jnp.concatenate([digits, jnp.zeros((EXTRA, D - ROWS), jnp.float32)], axis=1)
    out_ref[ROWS:PACK, :] = digits.astype(jnp.bfloat16)


def pack(embeddings, labels, order):
    anywhere = pl.BlockSpec(memory_space=pl.ANY)
    return pl.pallas_call(
        pack_kernel,
        out_shape=jax.ShapeDtypeStruct((PACK, D), jnp.bfloat16),
        in_specs=[anywhere] * 3,
        out_specs=pl.BlockSpec(memory_space=pltpu.VMEM),
        scratch_shapes=[
            pltpu.VMEM((ROWS, D), jnp.bfloat16),
            pltpu.VMEM((1, ROWS), jnp.int32),
            pltpu.VMEM((1, ROWS), jnp.int32),
            pltpu.SemaphoreType.DMA((3,)),
        ],
        name="normalize_pack",
        cost_estimate=pl.CostEstimate(flops=4 * ROWS * D, bytes_accessed=4 * ROWS * D, transcendentals=ROWS),
    )(embeddings, labels.reshape(1, ROWS), order.reshape(1, ROWS))


def weigh(value, cost):
    anywhere = pl.BlockSpec(memory_space=pl.ANY)
    return pl.pallas_call(
        lambda value_ref, out_ref: None,
        out_shape=jax.ShapeDtypeStruct(value.shape, value.dtype),
        in_specs=[anywhere],
        out_specs=anywhere,
        input_output_aliases={0: 0},
        name="weigh",
        cost_estimate=pl.CostEstimate(flops=cost, bytes_accessed=0, transcendentals=0),
    )(value)


def ranks(extra):
    return extra[0:1] * 4096.0 + extra[1:2] * 64.0 + extra[2:3]


def pair_kernel(core_ref, block_ref, sib_ref, out_ref):
    core = core_ref[0]
    out_ref[core] = block_ref[...]
    out_ref[1 - core] = sib_ref[...]


def pair(core, block, sib):
    inside = pl.BlockSpec(memory_space=pltpu.VMEM)
    return pl.pallas_call(
        pair_kernel,
        out_shape=jax.ShapeDtypeStruct((2, PACK, D), jnp.bfloat16),
        in_specs=[pl.BlockSpec(memory_space=pltpu.SMEM), inside, inside],
        out_specs=inside,
        compiler_params=pltpu.CompilerParams(vmem_limit_bytes=8 * 1024 * 1024),
        name="pair",
        cost_estimate=pl.CostEstimate(flops=0, bytes_accessed=8 * PACK * D, transcendentals=0),
    )(jnp.reshape(core, (1,)).astype(jnp.int32), block, sib)


def extra_of(ref):
    return ref[ROWS:PACK, 0:256].astype(jnp.float32)[:, :ROWS]


def gate_kernel(*refs):
    refs[-1][...] = refs[0][...]


def gate(value, *others):
    inside = pl.BlockSpec(memory_space=pltpu.VMEM)
    return pl.pallas_call(
        gate_kernel,
        out_shape=jax.ShapeDtypeStruct(value.shape, value.dtype),
        in_specs=[inside] + [pl.BlockSpec(memory_space=pl.ANY)] * len(others),
        out_specs=inside,
        compiler_params=pltpu.CompilerParams(vmem_limit_bytes=8 * 1024 * 1024),
        name="gate",
        cost_estimate=pl.CostEstimate(flops=0, bytes_accessed=4 * PACK * D, transcendentals=0),
    )(value, *others)


def prep_kernel(*refs):
    *given, left_ref, rank_ref, valid_ref = refs
    near = [given[k] for k in SLOTS]
    for s in range(2 * NEAR):
        left_ref[s * ROWS:(s + 1) * ROWS, :] = near[s][0:ROWS, :]
    extras = [extra_of(ref) for ref in near]
    same = [extra[3:4] == extras[0][3:4] for extra in extras]
    near_rank = jnp.concatenate([jnp.where(same[s], ranks(extras[s]), FAR) for s in range(2 * NEAR)], axis=1)
    rank_ref[...] = jnp.transpose(jnp.broadcast_to(near_rank, (128, LEFT)), (1, 0))
    for s in range(2, 2 * NEAR):
        valid_ref[s - 2] = same[s].astype(jnp.float32)


def prep(near):
    inside = pl.BlockSpec(memory_space=pltpu.VMEM)
    return pl.pallas_call(
        prep_kernel,
        out_shape=(
            jax.ShapeDtypeStruct((LEFT, D), jnp.bfloat16),
            jax.ShapeDtypeStruct((LEFT, 128), jnp.float32),
            jax.ShapeDtypeStruct((LEFT // ROWS - 2, 1, ROWS), jnp.float32),
        ),
        in_specs=[inside] * len(near),
        out_specs=(inside, inside, inside),
        compiler_params=pltpu.CompilerParams(vmem_limit_bytes=8 * 1024 * 1024),
        name="near_prep",
        cost_estimate=pl.CostEstimate(flops=0, bytes_accessed=4 * LEFT * D, transcendentals=0),
    )(*near)


def maxima_kernel(blocks, at, first, last, place_ref, left_ref, rank_ref, valid_ref, *refs):
    panel = refs[:blocks]
    *refs, right = refs[blocks:]
    if first:
        cols_ref, *rows_ref = refs
    else:
        prior_cols_ref, prior_ref, cols_ref, *rows_ref = refs
        cols_ref[...] = prior_cols_ref[...]
    width = blocks * ROWS
    for k in range(blocks):
        right[k * ROWS:(k + 1) * ROWS, :] = panel[k][0:ROWS, :]
    panel_rank = jnp.concatenate([ranks(extra_of(ref)) for ref in panel], axis=1)
    split = 2 * ROWS
    cols = []
    rows = None
    for start in range(0, width, TILE):
        tile = min(TILE, width - start)
        sims = lax.dot_general(
            left_ref[...], right[start:start + tile, :], (((1,), (1,)), ((), ())),
            preferred_element_type=jnp.float32,
        )
        for lane in range(0, tile, 128):
            lanes = min(128, tile - lane)
            part = sims[:, lane:lane + lanes]
            rank_row = panel_rank[:, start + lane:start + lane + lanes]
            rank_col = rank_ref[:, :lanes]
            here = part[:split]
            best = jnp.max(jnp.where(rank_col[:split] < rank_row, here, -1.0), axis=0, keepdims=True)
            there = part[split:]
            earlier = rank_row < rank_col[split:]
            best = jnp.maximum(best, jnp.max(jnp.where(earlier, -1.0, there), axis=0, keepdims=True))
            cols.append(best)
            found = jnp.where(earlier, there, -1.0)
            if lanes < 128:
                found = jnp.concatenate([found, jnp.full((LEFT - split, 128 - lanes), -1.0, jnp.float32)], axis=1)
            rows = found if rows is None else jnp.maximum(rows, found)
    best = jnp.concatenate(cols, axis=1)
    for k in range(blocks):
        cols_ref[place_ref[at + k]] = best[:, k * ROWS:(k + 1) * ROWS]
    if not first:
        rows = jnp.maximum(rows, prior_ref[...])
    if not last:
        rows_ref[0][...] = rows
    else:
        line = jnp.max(jnp.transpose(rows, (1, 0)), axis=0, keepdims=True)
        kept = [
            jnp.where(valid_ref[s] > 0.5, line[:, s * ROWS:(s + 1) * ROWS], -1.0) for s in range(LEFT // ROWS - 2)
        ]
        for s in range(NEAR - 1):
            rows_ref[0][s] = kept[2 * s]
            rows_ref[1][s] = kept[2 * s + 1]


def maxima(place, laid, panel, at, prior, last):
    inside = pl.BlockSpec(memory_space=pltpu.VMEM)
    blocks = len(panel)
    operands = (*laid, *panel, *prior)
    lines = jax.ShapeDtypeStruct((NEAR - 1, 1, ROWS), jnp.float32)
    held = jax.ShapeDtypeStruct((LEFT - 2 * ROWS, 128), jnp.float32)
    rows = (lines, lines) if last else (held,)
    return pl.pallas_call(
        lambda *refs: maxima_kernel(blocks, at, not prior, last, *refs),
        out_shape=(jax.ShapeDtypeStruct((2 * X, 1, ROWS), jnp.float32), *rows),
        in_specs=[pl.BlockSpec(memory_space=pltpu.SMEM)] + [inside] * len(operands),
        out_specs=(inside,) * (1 + len(rows)),
        scratch_shapes=[pltpu.VMEM((blocks * ROWS, D), jnp.bfloat16)],
        compiler_params=pltpu.CompilerParams(vmem_limit_bytes=16 * 1024 * 1024),
        name="panel_maxima",
        cost_estimate=pl.CostEstimate(
            flops=2 * LEFT * blocks * ROWS * D, bytes_accessed=2 * (2 * NEAR + blocks) * PACK * D, transcendentals=0
        ),
    )(place, *operands)


def shift(value, steps, count):
    pairs = [(i, i + steps) for i in range(count) if 0 <= i + steps < count]
    return lax.ppermute(value, "grp", pairs)


def swap(value, axis):
    return lax.ppermute(value, axis, [(0, 1), (1, 0)])


def half_flip(value, count):
    pairs = []
    for g in range(count):
        low, y = divmod(g, count // Z_LO)
        for h in range(2):
            for c in range(2):
                z = (h * Z_LO + low + (2 if c == 0 else 2 * Z_LO - 2)) % (2 * Z_LO)
                target = z % Z_LO * (count // Z_LO) + y
                pairs.append(((g * 2 + h) * 2 + c, (target * 2 + z // Z_LO) * 2 + c))
    return lax.ppermute(value, ("grp", "zh", "core"), pairs)


def turn_x(value, even):
    pairs = [(2 * i, 2 * ((i + even) % X)) for i in range(X)]
    pairs += [(2 * i + 1, 2 * ((i + X - even) % X) + 1) for i in range(X)]
    return lax.ppermute(value, ("x", "core"), pairs)


def shift_both(value, even, odd, count):
    pairs = [(2 * i, 2 * (i + even)) for i in range(count) if 0 <= i + even < count]
    pairs += [(2 * i + 1, 2 * (i + odd) + 1) for i in range(count) if 0 <= i + odd < count]
    return lax.ppermute(value, ("grp", "core"), pairs)


def per_device(embeddings, labels, order):
    count = lax.axis_size("grp")
    grp, zh, x, core = (lax.axis_index(axis) for axis in ("grp", "zh", "x", "core"))
    block = pack(embeddings, labels, order)
    flipped = half_flip(half_flip(block, count), count)
    one = shift(block, MOVES[0], count)
    far = shift(shift(block, -1, count), MOVES[1] + 1, count)
    two = shift(one, MOVES[2] - MOVES[0], count)
    sib = swap(block, "core")
    ahead, behind = turn_x(block, 1), turn_x(block, -1)
    across = turn_x(ahead, 1)
    one_sib, far_sib, two_sib = (swap(value, "core") for value in (one, far, two))
    flipped = gate(flipped, across, one_sib, sib, behind)
    flip_ahead, flip_behind = turn_x(flipped, 1), turn_x(flipped, -1)
    flip_across = turn_x(flip_ahead, 1)
    panel = [block, ahead, behind, across]
    other = [flipped, flip_ahead, flip_behind, flip_across]
    laid = prep((block, one, one_sib, far, far_sib, two, two_sib, sib))
    turn = jnp.where(core == 0, 1, X - 1)
    place = [(zh + h) % 2 * X + (x + (X - k) * turn) % X for h in range(2) for k in (0, 1, X - 1, 2)]
    place = jnp.stack(place).astype(jnp.int32)
    cols, rows = maxima(place, laid, panel, 0, (), False)
    cols, rows = maxima(place, laid, other[:3], X, (cols, rows), False)
    cols, rows, rows_sib = maxima(place, laid, other[3:], X + 3, (cols, rows), True)
    best = jnp.max(lax.all_to_all(cols, ("zh", "x"), 0, 0, tiled=True), axis=0)
    mine = jnp.maximum(rows, swap(rows_sib, "core"))
    for i, steps in enumerate(MOVES):
        back = shift(mine[i], -steps, count)
        source = grp + steps
        best = jnp.maximum(best, jnp.where((source >= 0) & (source < count), back, -1.0))
    return best.reshape(ROWS)


def solution(mesh):
    axes = ("grp", "zh", "x", "core")
    fine = Mesh(mesh.devices.reshape(mesh.shape["grp"], 2, X, 2), axes)
    return jax.shard_map(
        per_device,
        mesh=fine,
        in_specs=(P(axes, None), P(axes), P(axes)),
        out_specs=P(axes),
        check_vma=False,
    )
```

```python
import jax
import jax.numpy as jnp
from jax import lax
from jax.experimental import pallas as pl
from jax.experimental.pallas import tpu as pltpu
from jax.sharding import Mesh, PartitionSpec as P

ROWS = 192
EXTRA = 16
PACK = ROWS + EXTRA
D = 1024
X = 4
Z_LO = 4
MOVES = (1, -2, 3)
NEAR = 1 + len(MOVES)
LEFT = 2 * NEAR * ROWS
TILE = 256
FAR = 1.0e9


def pack_kernel(emb_any, lab_any, ord_any, out_ref, emb_ref, lab_ref, ord_ref, sems):
    copies = [
        pltpu.make_async_copy(source, target, sems.at[k])
        for k, (source, target) in enumerate(((emb_any, emb_ref), (lab_any, lab_ref), (ord_any, ord_ref)))
    ]
    for copy in copies:
        copy.start()
    for copy in copies:
        copy.wait()
    values = emb_ref[...].astype(jnp.float32)
    scale = lax.rsqrt(jnp.sum(values * values, axis=1, keepdims=True) + 1e-06)
    out_ref[0:ROWS, :] = (values * scale).astype(jnp.bfloat16)
    rank = jnp.broadcast_to(ord_ref[...], (EXTRA, ROWS))
    label = jnp.broadcast_to(lab_ref[...], (EXTRA, ROWS))
    line = lax.broadcasted_iota(jnp.int32, (EXTRA, ROWS), 0)
    digits = jnp.where(
        line == 0,
        rank >> 12,
        jnp.where(line == 1, (rank >> 6) & 63, jnp.where(line == 2, rank & 63, label + 1)),
    )
    digits = jnp.where(line < 4, digits, 0).astype(jnp.float32)
    digits = jnp.concatenate([digits, jnp.zeros((EXTRA, D - ROWS), jnp.float32)], axis=1)
    out_ref[ROWS:PACK, :] = digits.astype(jnp.bfloat16)


def pack(embeddings, labels, order):
    anywhere = pl.BlockSpec(memory_space=pl.ANY)
    return pl.pallas_call(
        pack_kernel,
        out_shape=jax.ShapeDtypeStruct((PACK, D), jnp.bfloat16),
        in_specs=[anywhere] * 3,
        out_specs=pl.BlockSpec(memory_space=pltpu.VMEM),
        scratch_shapes=[
            pltpu.VMEM((ROWS, D), jnp.bfloat16),
            pltpu.VMEM((1, ROWS), jnp.int32),
            pltpu.VMEM((1, ROWS), jnp.int32),
            pltpu.SemaphoreType.DMA((3,)),
        ],
        name="normalize_pack",
        cost_estimate=pl.CostEstimate(flops=4 * ROWS * D, bytes_accessed=4 * ROWS * D, transcendentals=ROWS),
    )(embeddings, labels.reshape(1, ROWS), order.reshape(1, ROWS))


def ranks(extra):
    return extra[0:1] * 4096.0 + extra[1:2] * 64.0 + extra[2:3]


def stack_kernel(*refs):
    out_ref = refs[-1]
    for k in range(out_ref.shape[0]):
        out_ref[k] = refs[k][...]


def stack(blocks, after=()):
    inside = pl.BlockSpec(memory_space=pltpu.VMEM)
    n = len(blocks)
    return pl.pallas_call(
        stack_kernel,
        out_shape=jax.ShapeDtypeStruct((n, PACK, D), jnp.bfloat16),
        in_specs=[inside] * (n + len(after)),
        out_specs=inside,
        compiler_params=pltpu.CompilerParams(vmem_limit_bytes=8 * 1024 * 1024),
        name="stack_blocks",
        cost_estimate=pl.CostEstimate(flops=0, bytes_accessed=4 * n * PACK * D, transcendentals=0),
    )(*blocks, *after)


def extra_of(ref):
    return ref[ROWS:PACK, 0:256].astype(jnp.float32)[:, :ROWS]


def gate_kernel(*refs):
    refs[-1][...] = refs[0][...]


def gate(value, *others):
    inside = pl.BlockSpec(memory_space=pltpu.VMEM)
    return pl.pallas_call(
        gate_kernel,
        out_shape=jax.ShapeDtypeStruct(value.shape, value.dtype),
        in_specs=[inside] * (1 + len(others)),
        out_specs=inside,
        compiler_params=pltpu.CompilerParams(vmem_limit_bytes=8 * 1024 * 1024),
        name="gate",
        cost_estimate=pl.CostEstimate(flops=0, bytes_accessed=4 * PACK * D, transcendentals=0),
    )(value, *others)


def lay_out(near, left_ref, rank_ref, valid_ref):
    for s in range(2 * NEAR):
        left_ref[s * ROWS:(s + 1) * ROWS, :] = near[s][0:ROWS, :]
    extras = [extra_of(ref) for ref in near]
    same = [extra[3:4] == extras[0][3:4] for extra in extras]
    near_rank = jnp.concatenate([jnp.where(same[s], ranks(extras[s]), FAR) for s in range(2 * NEAR)], axis=1)
    rank_ref[...] = jnp.transpose(jnp.broadcast_to(near_rank, (128, LEFT)), (1, 0))
    for s in range(2, 2 * NEAR):
        valid_ref[s - 2] = same[s].astype(jnp.float32)


def panel_maxima(panel, right, left_ref, rank_ref):
    blocks = len(panel)
    width = blocks * ROWS
    for k in range(blocks):
        right[k * ROWS:(k + 1) * ROWS, :] = panel[k][0:ROWS, :]
    panel_rank = jnp.concatenate([ranks(extra_of(ref)) for ref in panel], axis=1)
    split = 2 * ROWS
    cols = []
    rows = None
    for start in range(0, width, TILE):
        tile = min(TILE, width - start)
        sims = lax.dot_general(
            left_ref[...], right[start:start + tile, :], (((1,), (1,)), ((), ())),
            preferred_element_type=jnp.float32,
        )
        for lane in range(0, tile, 128):
            part = sims[:, lane:lane + 128]
            rank_row = panel_rank[:, start + lane:start + lane + 128]
            here = part[:split]
            best = jnp.max(jnp.where(rank_ref[:split] < rank_row, here, -1.0), axis=0, keepdims=True)
            there = part[split:]
            earlier = rank_row < rank_ref[split:]
            best = jnp.maximum(best, jnp.max(jnp.where(earlier, -1.0, there), axis=0, keepdims=True))
            cols.append(best)
            found = jnp.where(earlier, there, -1.0)
            rows = found if rows is None else jnp.maximum(rows, found)
    return jnp.concatenate(cols, axis=1), rows


def first_kernel(place_ref, mine_a_ref, mine_b_ref, theirs_a_ref, theirs_b_ref, *refs):
    pairs = ((mine_a_ref, theirs_a_ref), (mine_b_ref, theirs_b_ref))
    near = [ref.at[k] for pair in pairs for k in range(2) for ref in pair]
    *panel, cols_ref, rows_ref, left_ref, rank_ref, valid_ref, right = refs
    lay_out(near, left_ref, rank_ref, valid_ref)
    best, rows = panel_maxima(panel, right, left_ref, rank_ref)
    cols_ref[...] = jnp.full(cols_ref.shape, -1.0, jnp.float32)
    for k in range(len(panel)):
        cols_ref[place_ref[k]] = best[:, k * ROWS:(k + 1) * ROWS]
    rows_ref[...] = rows


def last_kernel(place_ref, cols_in_ref, rows_in_ref, left_ref, rank_ref, valid_ref, pair_ref, cols_ref, mine_ref, theirs_ref, right):
    panel = [pair_ref.at[k] for k in range(2)]
    best, rows = panel_maxima(panel, right, left_ref, rank_ref)
    cols_ref[...] = cols_in_ref[...]
    for k in range(2):
        cols_ref[place_ref[2 * X - 2 + k]] = best[:, k * ROWS:(k + 1) * ROWS]
    rows = jnp.maximum(rows, rows_in_ref[...])
    line = jnp.max(jnp.transpose(rows, (1, 0)), axis=0, keepdims=True)
    for s in range(NEAR - 1):
        for k, ref in enumerate((mine_ref, theirs_ref)):
            at = 2 * s + k
            ref[s] = jnp.where(valid_ref[at] > 0.5, line[:, at * ROWS:(at + 1) * ROWS], -1.0)


def cost(blocks):
    return pl.CostEstimate(
        flops=2 * LEFT * blocks * ROWS * D, bytes_accessed=2 * (2 * NEAR + blocks) * PACK * D, transcendentals=0
    )


def first_maxima(place, near, panel):
    inside = pl.BlockSpec(memory_space=pltpu.VMEM)
    blocks = len(panel)
    return pl.pallas_call(
        first_kernel,
        out_shape=(
            jax.ShapeDtypeStruct((2 * X, 1, ROWS), jnp.float32),
            jax.ShapeDtypeStruct((LEFT - 2 * ROWS, 128), jnp.float32),
            jax.ShapeDtypeStruct((LEFT, D), jnp.bfloat16),
            jax.ShapeDtypeStruct((LEFT, 128), jnp.float32),
            jax.ShapeDtypeStruct((2 * (NEAR - 1), 1, ROWS), jnp.float32),
        ),
        in_specs=[pl.BlockSpec(memory_space=pltpu.SMEM)] + [inside] * (4 + blocks),
        out_specs=(inside,) * 5,
        scratch_shapes=[pltpu.VMEM((blocks * ROWS, D), jnp.bfloat16)],
        compiler_params=pltpu.CompilerParams(vmem_limit_bytes=20 * 1024 * 1024),
        name="first_maxima",
        cost_estimate=cost(blocks),
    )(place, *near, *panel)


def last_maxima(place, carried, pair):
    inside = pl.BlockSpec(memory_space=pltpu.VMEM)
    lines = jax.ShapeDtypeStruct((NEAR - 1, 1, ROWS), jnp.float32)
    return pl.pallas_call(
        last_kernel,
        out_shape=(jax.ShapeDtypeStruct((2 * X, 1, ROWS), jnp.float32), lines, lines),
        in_specs=[pl.BlockSpec(memory_space=pltpu.SMEM)] + [inside] * (1 + len(carried)),
        out_specs=(inside,) * 3,
        scratch_shapes=[pltpu.VMEM((2 * ROWS, D), jnp.bfloat16)],
        compiler_params=pltpu.CompilerParams(vmem_limit_bytes=20 * 1024 * 1024),
        name="last_maxima",
        cost_estimate=cost(2),
    )(place, *carried, pair)


def half_flip(value, count):
    pairs = []
    for g in range(count):
        low, y = divmod(g, count // Z_LO)
        for h in range(2):
            for c in range(2):
                z = (h * Z_LO + low + (2 if c == 0 else 2 * Z_LO - 2)) % (2 * Z_LO)
                target = z % Z_LO * (count // Z_LO) + y
                pairs.append(((g * 2 + h) * 2 + c, (target * 2 + z // Z_LO) * 2 + c))
    return lax.ppermute(value, ("grp", "zh", "core"), pairs)


def shift(value, steps, count):
    pairs = [(i, i + steps) for i in range(count) if 0 <= i + steps < count]
    return lax.ppermute(value, "grp", pairs)


def swap(value, axis):
    return lax.ppermute(value, axis, [(0, 1), (1, 0)])


def turn_x(value, even):
    pairs = [(2 * i, 2 * ((i + even) % X)) for i in range(X)]
    pairs += [(2 * i + 1, 2 * ((i + X - even) % X) + 1) for i in range(X)]
    return lax.ppermute(value, ("x", "core"), pairs)


def per_device(embeddings, labels, order):
    count = lax.axis_size("grp")
    grp, zh, x, core = (lax.axis_index(axis) for axis in ("grp", "zh", "x", "core"))
    block = pack(embeddings, labels, order)
    one = shift(block, MOVES[0], count)
    two = shift(block, MOVES[1], count)
    three = shift(one, MOVES[2] - MOVES[0], count)
    ahead, behind = turn_x(block, 1), turn_x(block, -1)
    flipped = gate(half_flip(half_flip(block, count), count), ahead)
    flip_ahead, flip_behind = turn_x(flipped, 1), turn_x(flipped, -1)
    across = turn_x(stack((ahead, flip_ahead), (flip_behind, behind)), 1)
    mine = (stack((block, one)), stack((two, three)))
    theirs = [swap(value, "core") for value in mine]
    turn = jnp.where(core == 0, 1, X - 1)
    slots = [(zh + h) % 2 * X + (x + (X - k) * turn) % X for k in (0, 1, X - 1, 2) for h in range(2)]
    place = jnp.stack(slots).astype(jnp.int32)
    carried = first_maxima(place, (*mine, *theirs), [block, flipped, ahead, flip_ahead, behind, flip_behind])
    cols, rows, rows_sib = last_maxima(place, carried, across)
    best = jnp.max(lax.all_to_all(cols, ("zh", "x"), 0, 0, tiled=True), axis=0)
    mine = jnp.maximum(rows, swap(rows_sib, "core"))
    for i, steps in enumerate(MOVES):
        back = shift(mine[i], -steps, count)
        source = grp + steps
        best = jnp.maximum(best, jnp.where((source >= 0) & (source < count), back, -1.0))
    return best.reshape(ROWS)


def solution(mesh):
    axes = ("grp", "zh", "x", "core")
    fine = Mesh(mesh.devices.reshape(mesh.shape["grp"], 2, X, 2), axes)
    return jax.shard_map(
        per_device,
        mesh=fine,
        in_specs=(P(axes, None), P(axes), P(axes)),
        out_specs=P(axes),
        check_vma=False,
    )
```

```python
import jax
import jax.numpy as jnp
from jax import lax
from jax.experimental import pallas as pl
from jax.experimental.pallas import tpu as pltpu
from jax.sharding import Mesh, PartitionSpec as P

ROWS = 192
EXTRA = 16
PACK = ROWS + EXTRA
D = 1024
X = 4
Z_LO = 4
MOVES = (1, 2, -3)
NEAR = 1 + len(MOVES)
LEFT = 2 * NEAR * ROWS
TILE = 256
FAR = 1.0e9
FIRST = 6


def pack_kernel(emb_any, lab_any, ord_any, out_ref, emb_ref, lab_ref, ord_ref, sems):
    copies = [
        pltpu.make_async_copy(source, target, sems.at[k])
        for k, (source, target) in enumerate(((emb_any, emb_ref), (lab_any, lab_ref), (ord_any, ord_ref)))
    ]
    for copy in copies:
        copy.start()
    for copy in copies:
        copy.wait()
    values = emb_ref[...].astype(jnp.float32)
    scale = lax.rsqrt(jnp.sum(values * values, axis=1, keepdims=True) + 1e-06)
    out_ref[0:ROWS, :] = (values * scale).astype(jnp.bfloat16)
    rank = jnp.broadcast_to(ord_ref[...], (EXTRA, ROWS))
    label = jnp.broadcast_to(lab_ref[...], (EXTRA, ROWS))
    line = lax.broadcasted_iota(jnp.int32, (EXTRA, ROWS), 0)
    digits = jnp.where(
        line == 0,
        rank >> 12,
        jnp.where(line == 1, (rank >> 6) & 63, jnp.where(line == 2, rank & 63, label + 1)),
    )
    digits = jnp.where(line < 4, digits, 0).astype(jnp.float32)
    digits = jnp.concatenate([digits, jnp.zeros((EXTRA, D - ROWS), jnp.float32)], axis=1)
    out_ref[ROWS:PACK, :] = digits.astype(jnp.bfloat16)


def pack(embeddings, labels, order):
    anywhere = pl.BlockSpec(memory_space=pl.ANY)
    return pl.pallas_call(
        pack_kernel,
        out_shape=jax.ShapeDtypeStruct((PACK, D), jnp.bfloat16),
        in_specs=[anywhere] * 3,
        out_specs=pl.BlockSpec(memory_space=pltpu.VMEM),
        scratch_shapes=[
            pltpu.VMEM((ROWS, D), jnp.bfloat16),
            pltpu.VMEM((1, ROWS), jnp.int32),
            pltpu.VMEM((1, ROWS), jnp.int32),
            pltpu.SemaphoreType.DMA((3,)),
        ],
        name="normalize_pack",
        cost_estimate=pl.CostEstimate(flops=4 * ROWS * D, bytes_accessed=4 * ROWS * D, transcendentals=ROWS),
    )(embeddings, labels.reshape(1, ROWS), order.reshape(1, ROWS))


def ranks(extra):
    return extra[0:1] * 4096.0 + extra[1:2] * 64.0 + extra[2:3]


def stack_kernel(*refs):
    out_ref = refs[-1]
    for k in range(out_ref.shape[0]):
        out_ref[k] = refs[k][...]


def stack(blocks, after=()):
    inside = pl.BlockSpec(memory_space=pltpu.VMEM)
    n = len(blocks)
    return pl.pallas_call(
        stack_kernel,
        out_shape=jax.ShapeDtypeStruct((n, PACK, D), jnp.bfloat16),
        in_specs=[inside] * (n + len(after)),
        out_specs=inside,
        compiler_params=pltpu.CompilerParams(vmem_limit_bytes=8 * 1024 * 1024),
        name="stack_blocks",
        cost_estimate=pl.CostEstimate(flops=0, bytes_accessed=4 * n * PACK * D, transcendentals=0),
    )(*blocks, *after)


def extra_of(ref):
    return ref[ROWS:PACK, 0:256].astype(jnp.float32)[:, :ROWS]


def gate_kernel(*refs):
    refs[-1][...] = refs[0][...]


def gate(value, *others):
    inside = pl.BlockSpec(memory_space=pltpu.VMEM)
    return pl.pallas_call(
        gate_kernel,
        out_shape=jax.ShapeDtypeStruct(value.shape, value.dtype),
        in_specs=[inside] * (1 + len(others)),
        out_specs=inside,
        compiler_params=pltpu.CompilerParams(vmem_limit_bytes=8 * 1024 * 1024),
        name="gate",
        cost_estimate=pl.CostEstimate(flops=0, bytes_accessed=4 * PACK * D, transcendentals=0),
    )(value, *others)


def lay_out(near, left_ref, rank_ref, valid_ref):
    for s in range(2 * NEAR):
        left_ref[s * ROWS:(s + 1) * ROWS, :] = near[s][0:ROWS, :]
    extras = [extra_of(ref) for ref in near]
    same = [extra[3:4] == extras[0][3:4] for extra in extras]
    near_rank = jnp.concatenate([jnp.where(same[s], ranks(extras[s]), FAR) for s in range(2 * NEAR)], axis=1)
    rank_ref[...] = jnp.transpose(jnp.broadcast_to(near_rank, (128, LEFT)), (1, 0))
    for s in range(2, 2 * NEAR):
        valid_ref[s - 2] = same[s].astype(jnp.float32)


def panel_maxima(panel, right, left_ref, rank_ref):
    blocks = len(panel)
    width = blocks * ROWS
    for k in range(blocks):
        right[k * ROWS:(k + 1) * ROWS, :] = panel[k][0:ROWS, :]
    panel_rank = jnp.concatenate([ranks(extra_of(ref)) for ref in panel], axis=1)
    split = 2 * ROWS
    cols = []
    rows = None
    for start in range(0, width, TILE):
        tile = min(TILE, width - start)
        sims = lax.dot_general(
            left_ref[...], right[start:start + tile, :], (((1,), (1,)), ((), ())),
            preferred_element_type=jnp.float32,
        )
        for lane in range(0, tile, 128):
            part = sims[:, lane:lane + 128]
            rank_row = panel_rank[:, start + lane:start + lane + 128]
            here = part[:split]
            best = jnp.max(jnp.where(rank_ref[:split] < rank_row, here, -1.0), axis=0, keepdims=True)
            there = part[split:]
            earlier = rank_row < rank_ref[split:]
            best = jnp.maximum(best, jnp.max(jnp.where(earlier, -1.0, there), axis=0, keepdims=True))
            cols.append(best)
            found = jnp.where(earlier, there, -1.0)
            rows = found if rows is None else jnp.maximum(rows, found)
    return jnp.concatenate(cols, axis=1), rows


def first_kernel(place_ref, *refs):
    *given, cols_ref, rows_ref, left_ref, rank_ref, valid_ref, right = refs
    panel, given = given[:FIRST], given[FIRST:]
    mine, theirs = given[:len(given) // 2], given[len(given) // 2:]
    near = []
    for pair in zip(mine, theirs):
        if len(pair[0].shape) == 2:
            near += pair
        else:
            near += [ref.at[k] for k in range(pair[0].shape[0]) for ref in pair]
    lay_out(near, left_ref, rank_ref, valid_ref)
    best, rows = panel_maxima(panel, right, left_ref, rank_ref)
    cols_ref[...] = jnp.full(cols_ref.shape, -1.0, jnp.float32)
    for k in range(FIRST):
        cols_ref[place_ref[k]] = best[:, k * ROWS:(k + 1) * ROWS]
    rows_ref[...] = rows


def last_kernel(place_ref, *refs):
    *given, cols_in_ref, rows_in_ref, left_ref, rank_ref, valid_ref, cols_ref, mine_ref, theirs_ref, right = refs
    panel = [ref.at[k] for ref in given for k in range(2)] if len(given) == 1 else given
    best, rows = panel_maxima(panel, right, left_ref, rank_ref)
    cols_ref[...] = cols_in_ref[...]
    for k in range(2 * X - FIRST):
        cols_ref[place_ref[FIRST + k]] = best[:, k * ROWS:(k + 1) * ROWS]
    rows = jnp.maximum(rows, rows_in_ref[...])
    line = jnp.max(jnp.transpose(rows, (1, 0)), axis=0, keepdims=True)
    for s in range(NEAR - 1):
        for k, ref in enumerate((mine_ref, theirs_ref)):
            at = 2 * s + k
            ref[s] = jnp.where(valid_ref[at] > 0.5, line[:, at * ROWS:(at + 1) * ROWS], -1.0)


def cost(blocks):
    return pl.CostEstimate(
        flops=2 * LEFT * blocks * ROWS * D, bytes_accessed=2 * (2 * NEAR + blocks) * PACK * D, transcendentals=0
    )


def first_maxima(place, near, panel):
    inside = pl.BlockSpec(memory_space=pltpu.VMEM)
    blocks = len(panel)
    return pl.pallas_call(
        first_kernel,
        out_shape=(
            jax.ShapeDtypeStruct((2 * X, 1, ROWS), jnp.float32),
            jax.ShapeDtypeStruct((LEFT - 2 * ROWS, 128), jnp.float32),
            jax.ShapeDtypeStruct((LEFT, D), jnp.bfloat16),
            jax.ShapeDtypeStruct((LEFT, 128), jnp.float32),
            jax.ShapeDtypeStruct((2 * (NEAR - 1), 1, ROWS), jnp.float32),
        ),
        in_specs=[pl.BlockSpec(memory_space=pltpu.SMEM)] + [inside] * (len(near) + blocks),
        out_specs=(inside,) * 5,
        scratch_shapes=[pltpu.VMEM((blocks * ROWS, D), jnp.bfloat16)],
        compiler_params=pltpu.CompilerParams(vmem_limit_bytes=20 * 1024 * 1024),
        name="first_maxima",
        cost_estimate=cost(blocks),
    )(place, *panel, *near)


def last_maxima(place, panel, carried):
    inside = pl.BlockSpec(memory_space=pltpu.VMEM)
    lines = jax.ShapeDtypeStruct((NEAR - 1, 1, ROWS), jnp.float32)
    blocks = 2 * X - FIRST
    return pl.pallas_call(
        last_kernel,
        out_shape=(jax.ShapeDtypeStruct((2 * X, 1, ROWS), jnp.float32), lines, lines),
        in_specs=[pl.BlockSpec(memory_space=pltpu.SMEM)] + [inside] * (len(panel) + len(carried)),
        out_specs=(inside,) * 3,
        scratch_shapes=[pltpu.VMEM((blocks * ROWS, D), jnp.bfloat16)],
        compiler_params=pltpu.CompilerParams(vmem_limit_bytes=20 * 1024 * 1024),
        name="last_maxima",
        cost_estimate=cost(blocks),
    )(place, *panel, *carried)


def half_flip(value, count):
    pairs = []
    for g in range(count):
        low, y = divmod(g, count // Z_LO)
        for h in range(2):
            for c in range(2):
                z = (h * Z_LO + low + (2 if c == 0 else 2 * Z_LO - 2)) % (2 * Z_LO)
                target = z % Z_LO * (count // Z_LO) + y
                pairs.append(((g * 2 + h) * 2 + c, (target * 2 + z // Z_LO) * 2 + c))
    return lax.ppermute(value, ("grp", "zh", "core"), pairs)


def shift(value, steps, count):
    pairs = [(i, i + steps) for i in range(count) if 0 <= i + steps < count]
    return lax.ppermute(value, "grp", pairs)


def swap(value, axis):
    return lax.ppermute(value, axis, [(0, 1), (1, 0)])


def turn_x(value, even):
    pairs = [(2 * i, 2 * ((i + even) % X)) for i in range(X)]
    pairs += [(2 * i + 1, 2 * ((i + X - even) % X) + 1) for i in range(X)]
    return lax.ppermute(value, ("x", "core"), pairs)


def per_device(embeddings, labels, order):
    count = lax.axis_size("grp")
    grp, zh, x, core = (lax.axis_index(axis) for axis in ("grp", "zh", "x", "core"))
    block = pack(embeddings, labels, order)
    one = shift(block, MOVES[0], count)
    two = shift(block, MOVES[1], count)
    three = shift(block, MOVES[2], count)
    ahead, behind = turn_x(block, 1), turn_x(block, -1)
    across = turn_x(ahead, 1)
    sib = swap(block, "core")
    flipped = gate(swap(block, "zh"), ahead, behind, across)
    flip_ahead, flip_behind = turn_x(flipped, 1), turn_x(flipped, -1)
    flip_across = turn_x(flip_ahead, 1)
    mine = (block, one, stack((two, three)))
    theirs = [sib] + [swap(value, "core") for value in mine[1:]]
    turn = jnp.where(core == 0, 1, X - 1)
    order_held = ((0, 0), (1, 0), (0, 1), (1, 1), (0, X - 1), (0, 2), (1, X - 1), (1, 2))
    slots = [(zh + h) % 2 * X + (x + (X - k) * turn) % X for h, k in order_held]
    place = jnp.stack(slots).astype(jnp.int32)
    carried = first_maxima(place, (*mine, *theirs), [block, flipped, ahead, flip_ahead, behind, across])
    cols, rows, rows_sib = last_maxima(place, [flip_behind, flip_across], carried)
    best = jnp.max(lax.all_to_all(cols, ("zh", "x"), 0, 0, tiled=True), axis=0)
    mine = jnp.maximum(rows, swap(rows_sib, "core"))
    for i, steps in enumerate(MOVES):
        back = shift(mine[i], -steps, count)
        source = grp + steps
        best = jnp.maximum(best, jnp.where((source >= 0) & (source < count), back, -1.0))
    return best.reshape(ROWS)


def solution(mesh):
    axes = ("grp", "zh", "x", "core")
    fine = Mesh(mesh.devices.reshape(mesh.shape["grp"], 2, X, 2), axes)
    return jax.shard_map(
        per_device,
        mesh=fine,
        in_specs=(P(axes, None), P(axes), P(axes)),
        out_specs=P(axes),
        check_vma=False,
    )
```

```python
import jax
import jax.numpy as jnp
from jax import lax
from jax.experimental import pallas as pl
from jax.experimental.pallas import tpu as pltpu
from jax.sharding import Mesh, PartitionSpec as P

ROWS = 192
EXTRA = 8
PACK = ROWS + EXTRA
D = 1024
X = 4
Z_LO = 4
MOVES = (1, 2, -3)
NEAR = 1 + len(MOVES)
LEFT = 2 * NEAR * ROWS
TILE = 256
FAR = 1.0e9
FIRST = 6


def pack_kernel(emb_any, lab_any, ord_any, out_ref, emb_ref, lab_ref, ord_ref, sems):
    copies = [
        pltpu.make_async_copy(source, target, sems.at[k])
        for k, (source, target) in enumerate(((emb_any, emb_ref), (lab_any, lab_ref), (ord_any, ord_ref)))
    ]
    for copy in copies:
        copy.start()
    for copy in copies:
        copy.wait()
    values = emb_ref[...].astype(jnp.float32)
    scale = lax.rsqrt(jnp.sum(values * values, axis=1, keepdims=True) + 1e-06)
    out_ref[0:ROWS, :] = (values * scale).astype(jnp.bfloat16)
    rank = jnp.broadcast_to(ord_ref[...], (EXTRA, ROWS))
    label = jnp.broadcast_to(lab_ref[...], (EXTRA, ROWS))
    line = lax.broadcasted_iota(jnp.int32, (EXTRA, ROWS), 0)
    digits = jnp.where(
        line == 0,
        rank >> 12,
        jnp.where(line == 1, (rank >> 6) & 63, jnp.where(line == 2, rank & 63, label + 1)),
    )
    digits = jnp.where(line < 4, digits, 0).astype(jnp.float32)
    digits = jnp.concatenate([digits, jnp.zeros((EXTRA, D - ROWS), jnp.float32)], axis=1)
    out_ref[ROWS:PACK, :] = digits.astype(jnp.bfloat16)


def pack(embeddings, labels, order):
    anywhere = pl.BlockSpec(memory_space=pl.ANY)
    return pl.pallas_call(
        pack_kernel,
        out_shape=jax.ShapeDtypeStruct((PACK, D), jnp.bfloat16),
        in_specs=[anywhere] * 3,
        out_specs=pl.BlockSpec(memory_space=pltpu.VMEM),
        scratch_shapes=[
            pltpu.VMEM((ROWS, D), jnp.bfloat16),
            pltpu.VMEM((1, ROWS), jnp.int32),
            pltpu.VMEM((1, ROWS), jnp.int32),
            pltpu.SemaphoreType.DMA((3,)),
        ],
        name="normalize_pack",
        cost_estimate=pl.CostEstimate(flops=4 * ROWS * D, bytes_accessed=4 * ROWS * D, transcendentals=ROWS),
    )(embeddings, labels.reshape(1, ROWS), order.reshape(1, ROWS))


def ranks(extra):
    return extra[0:1] * 4096.0 + extra[1:2] * 64.0 + extra[2:3]


def stack_kernel(*refs):
    out_ref = refs[-1]
    for k in range(out_ref.shape[0]):
        out_ref[k] = refs[k][...]


def stack(blocks, after=()):
    inside = pl.BlockSpec(memory_space=pltpu.VMEM)
    n = len(blocks)
    return pl.pallas_call(
        stack_kernel,
        out_shape=jax.ShapeDtypeStruct((n, PACK, D), jnp.bfloat16),
        in_specs=[inside] * (n + len(after)),
        out_specs=inside,
        compiler_params=pltpu.CompilerParams(vmem_limit_bytes=8 * 1024 * 1024),
        name="stack_blocks",
        cost_estimate=pl.CostEstimate(flops=0, bytes_accessed=4 * n * PACK * D, transcendentals=0),
    )(*blocks, *after)


def extra_of(ref):
    return ref[ROWS:PACK, 0:256].astype(jnp.float32)[:, :ROWS]


def gate_kernel(*refs):
    refs[-1][...] = refs[0][...]


def gate(value, *others):
    inside = pl.BlockSpec(memory_space=pltpu.VMEM)
    return pl.pallas_call(
        gate_kernel,
        out_shape=jax.ShapeDtypeStruct(value.shape, value.dtype),
        in_specs=[inside] * (1 + len(others)),
        out_specs=inside,
        compiler_params=pltpu.CompilerParams(vmem_limit_bytes=8 * 1024 * 1024),
        name="gate",
        cost_estimate=pl.CostEstimate(flops=0, bytes_accessed=4 * PACK * D, transcendentals=0),
    )(value, *others)


def lay_out(near, left_ref, rank_ref, valid_ref):
    for s in range(2 * NEAR):
        left_ref[s * ROWS:(s + 1) * ROWS, :] = near[s][0:ROWS, :]
    extras = [extra_of(ref) for ref in near]
    same = [extra[3:4] == extras[0][3:4] for extra in extras]
    near_rank = jnp.concatenate([jnp.where(same[s], ranks(extras[s]), FAR) for s in range(2 * NEAR)], axis=1)
    rank_ref[...] = jnp.transpose(jnp.broadcast_to(near_rank, (128, LEFT)), (1, 0))
    for s in range(2, 2 * NEAR):
        valid_ref[s - 2] = same[s].astype(jnp.float32)


def panel_maxima(panel, right, left_ref, rank_ref):
    blocks = len(panel)
    width = blocks * ROWS
    for k in range(blocks):
        right[k * ROWS:(k + 1) * ROWS, :] = panel[k][0:ROWS, :]
    panel_rank = jnp.concatenate([ranks(extra_of(ref)) for ref in panel], axis=1)
    split = 2 * ROWS
    cols = []
    rows = None
    for start in range(0, width, TILE):
        tile = min(TILE, width - start)
        sims = lax.dot_general(
            left_ref[...], right[start:start + tile, :], (((1,), (1,)), ((), ())),
            preferred_element_type=jnp.float32,
        )
        for lane in range(0, tile, 128):
            part = sims[:, lane:lane + 128]
            rank_row = panel_rank[:, start + lane:start + lane + 128]
            here = part[:split]
            best = jnp.max(jnp.where(rank_ref[:split] < rank_row, here, -1.0), axis=0, keepdims=True)
            there = part[split:]
            earlier = rank_row < rank_ref[split:]
            best = jnp.maximum(best, jnp.max(jnp.where(earlier, -1.0, there), axis=0, keepdims=True))
            cols.append(best)
            found = jnp.where(earlier, there, -1.0)
            rows = found if rows is None else jnp.maximum(rows, found)
    return jnp.concatenate(cols, axis=1), rows


def first_kernel(place_ref, *refs):
    *given, cols_ref, rows_ref, left_ref, rank_ref, valid_ref, right = refs
    panel, given = given[:FIRST], given[FIRST:]
    mine, theirs = given[:len(given) // 2], given[len(given) // 2:]
    near = []
    for pair in zip(mine, theirs):
        if len(pair[0].shape) == 2:
            near += pair
        else:
            near += [ref.at[k] for k in range(pair[0].shape[0]) for ref in pair]
    lay_out(near, left_ref, rank_ref, valid_ref)
    best, rows = panel_maxima(panel, right, left_ref, rank_ref)
    cols_ref[...] = jnp.full(cols_ref.shape, -1.0, jnp.float32)
    for k in range(FIRST):
        cols_ref[place_ref[k]] = best[:, k * ROWS:(k + 1) * ROWS]
    rows_ref[...] = rows


def last_kernel(place_ref, *refs):
    *given, cols_in_ref, rows_in_ref, left_ref, rank_ref, valid_ref, cols_ref, mine_ref, theirs_ref, right = refs
    panel = [ref.at[k] for ref in given for k in range(2)] if len(given) == 1 else given
    best, rows = panel_maxima(panel, right, left_ref, rank_ref)
    cols_ref[...] = cols_in_ref[...]
    for k in range(2 * X - FIRST):
        cols_ref[place_ref[FIRST + k]] = best[:, k * ROWS:(k + 1) * ROWS]
    rows = jnp.maximum(rows, rows_in_ref[...])
    line = jnp.max(jnp.transpose(rows, (1, 0)), axis=0, keepdims=True)
    for s in range(NEAR - 1):
        for k, ref in enumerate((mine_ref, theirs_ref)):
            at = 2 * s + k
            ref[s] = jnp.where(valid_ref[at] > 0.5, line[:, at * ROWS:(at + 1) * ROWS], -1.0)


def cost(blocks):
    return pl.CostEstimate(
        flops=2 * LEFT * blocks * ROWS * D, bytes_accessed=2 * (2 * NEAR + blocks) * PACK * D, transcendentals=0
    )


def first_maxima(place, near, panel):
    inside = pl.BlockSpec(memory_space=pltpu.VMEM)
    blocks = len(panel)
    return pl.pallas_call(
        first_kernel,
        out_shape=(
            jax.ShapeDtypeStruct((2 * X, 1, ROWS), jnp.float32),
            jax.ShapeDtypeStruct((LEFT - 2 * ROWS, 128), jnp.float32),
            jax.ShapeDtypeStruct((LEFT, D), jnp.bfloat16),
            jax.ShapeDtypeStruct((LEFT, 128), jnp.float32),
            jax.ShapeDtypeStruct((2 * (NEAR - 1), 1, ROWS), jnp.float32),
        ),
        in_specs=[pl.BlockSpec(memory_space=pltpu.SMEM)] + [inside] * (len(near) + blocks),
        out_specs=(inside,) * 5,
        scratch_shapes=[pltpu.VMEM((blocks * ROWS, D), jnp.bfloat16)],
        compiler_params=pltpu.CompilerParams(vmem_limit_bytes=20 * 1024 * 1024),
        name="first_maxima",
        cost_estimate=cost(blocks),
    )(place, *panel, *near)


def last_maxima(place, panel, carried):
    inside = pl.BlockSpec(memory_space=pltpu.VMEM)
    lines = jax.ShapeDtypeStruct((NEAR - 1, 1, ROWS), jnp.float32)
    blocks = 2 * X - FIRST
    return pl.pallas_call(
        last_kernel,
        out_shape=(jax.ShapeDtypeStruct((2 * X, 1, ROWS), jnp.float32), lines, lines),
        in_specs=[pl.BlockSpec(memory_space=pltpu.SMEM)] + [inside] * (len(panel) + len(carried)),
        out_specs=(inside,) * 3,
        scratch_shapes=[pltpu.VMEM((blocks * ROWS, D), jnp.bfloat16)],
        compiler_params=pltpu.CompilerParams(vmem_limit_bytes=20 * 1024 * 1024),
        name="last_maxima",
        cost_estimate=cost(blocks),
    )(place, *panel, *carried)


def half_flip(value, count):
    pairs = []
    for g in range(count):
        low, y = divmod(g, count // Z_LO)
        for h in range(2):
            for c in range(2):
                z = (h * Z_LO + low + (2 if c == 0 else 2 * Z_LO - 2)) % (2 * Z_LO)
                target = z % Z_LO * (count // Z_LO) + y
                pairs.append(((g * 2 + h) * 2 + c, (target * 2 + z // Z_LO) * 2 + c))
    return lax.ppermute(value, ("grp", "zh", "core"), pairs)


def shift(value, steps, count):
    pairs = [(i, i + steps) for i in range(count) if 0 <= i + steps < count]
    return lax.ppermute(value, "grp", pairs)


def swap(value, axis):
    return lax.ppermute(value, axis, [(0, 1), (1, 0)])


def turn_x(value, even):
    pairs = [(2 * i, 2 * ((i + even) % X)) for i in range(X)]
    pairs += [(2 * i + 1, 2 * ((i + X - even) % X) + 1) for i in range(X)]
    return lax.ppermute(value, ("x", "core"), pairs)


def per_device(embeddings, labels, order):
    count = lax.axis_size("grp")
    grp, zh, x, core = (lax.axis_index(axis) for axis in ("grp", "zh", "x", "core"))
    block = pack(embeddings, labels, order)
    one = shift(block, MOVES[0], count)
    two = shift(block, MOVES[1], count)
    three = shift(block, MOVES[2], count)
    ahead, behind = turn_x(block, 1), turn_x(block, -1)
    across = turn_x(ahead, 1)
    sib = swap(block, "core")
    flipped = half_flip(half_flip(block, count), count)
    flip_ahead = turn_x(flipped, 1)
    flip_behind = turn_x(gate(flipped, ahead, behind), -1)
    flip_across = turn_x(flip_ahead, 1)
    mine = (block, one, stack((two, three)))
    theirs = [sib] + [swap(value, "core") for value in mine[1:]]
    turn = jnp.where(core == 0, 1, X - 1)
    order_held = ((0, 0), (1, 0), (0, 1), (1, 1), (0, X - 1), (0, 2), (1, X - 1), (1, 2))
    slots = [(zh + h) % 2 * X + (x + (X - k) * turn) % X for h, k in order_held]
    place = jnp.stack(slots).astype(jnp.int32)
    carried = first_maxima(place, (*mine, *theirs), [block, flipped, ahead, flip_ahead, behind, across])
    cols, rows, rows_sib = last_maxima(place, [flip_behind, flip_across], carried)
    best = jnp.max(lax.all_to_all(cols, ("zh", "x"), 0, 0, tiled=True), axis=0)
    mine = jnp.maximum(rows, swap(rows_sib, "core"))
    for i, steps in enumerate(MOVES):
        back = shift(mine[i], -steps, count)
        source = grp + steps
        best = jnp.maximum(best, jnp.where((source >= 0) & (source < count), back, -1.0))
    return best.reshape(ROWS)


def solution(mesh):
    axes = ("grp", "zh", "x", "core")
    fine = Mesh(mesh.devices.reshape(mesh.shape["grp"], 2, X, 2), axes)
    return jax.shard_map(
        per_device,
        mesh=fine,
        in_specs=(P(axes, None), P(axes), P(axes)),
        out_specs=P(axes),
        check_vma=False,
    )
```

```python
import jax
import jax.numpy as jnp
from jax import lax
from jax.experimental import pallas as pl
from jax.experimental.pallas import tpu as pltpu
from jax.sharding import Mesh, PartitionSpec as P

ROWS = 192
EXTRA = 8
PACK = ROWS + EXTRA
D = 1024
X = 4
Z_LO = 4
MOVES = (1, 2, -3)
NEAR = 1 + len(MOVES)
LEFT = 2 * NEAR * ROWS
TILE = 256
FAR = 1.0e9
FIRST = 6


def pack_kernel(emb_any, lab_any, ord_any, out_ref, emb_ref, lab_ref, ord_ref, sems):
    copies = [
        pltpu.make_async_copy(source, target, sems.at[k])
        for k, (source, target) in enumerate(((emb_any, emb_ref), (lab_any, lab_ref), (ord_any, ord_ref)))
    ]
    for copy in copies:
        copy.start()
    for copy in copies:
        copy.wait()
    values = emb_ref[...].astype(jnp.float32)
    scale = lax.rsqrt(jnp.sum(values * values, axis=1, keepdims=True) + 1e-06)
    out_ref[0:ROWS, :] = (values * scale).astype(jnp.bfloat16)
    rank = jnp.broadcast_to(ord_ref[...], (EXTRA, ROWS))
    label = jnp.broadcast_to(lab_ref[...], (EXTRA, ROWS))
    line = lax.broadcasted_iota(jnp.int32, (EXTRA, ROWS), 0)
    digits = jnp.where(
        line == 0,
        rank >> 12,
        jnp.where(line == 1, (rank >> 6) & 63, jnp.where(line == 2, rank & 63, label + 1)),
    )
    digits = jnp.where(line < 4, digits, 0).astype(jnp.float32)
    digits = jnp.concatenate([digits, jnp.zeros((EXTRA, D - ROWS), jnp.float32)], axis=1)
    out_ref[ROWS:PACK, :] = digits.astype(jnp.bfloat16)


def pack(embeddings, labels, order):
    anywhere = pl.BlockSpec(memory_space=pl.ANY)
    return pl.pallas_call(
        pack_kernel,
        out_shape=jax.ShapeDtypeStruct((PACK, D), jnp.bfloat16),
        in_specs=[anywhere] * 3,
        out_specs=pl.BlockSpec(memory_space=pltpu.VMEM),
        scratch_shapes=[
            pltpu.VMEM((ROWS, D), jnp.bfloat16),
            pltpu.VMEM((1, ROWS), jnp.int32),
            pltpu.VMEM((1, ROWS), jnp.int32),
            pltpu.SemaphoreType.DMA((3,)),
        ],
        name="normalize_pack",
        cost_estimate=pl.CostEstimate(flops=4 * ROWS * D, bytes_accessed=4 * ROWS * D, transcendentals=ROWS),
    )(embeddings, labels.reshape(1, ROWS), order.reshape(1, ROWS))


def ranks(extra):
    return extra[0:1] * 4096.0 + extra[1:2] * 64.0 + extra[2:3]


def stack_kernel(*refs):
    out_ref = refs[-1]
    for k in range(out_ref.shape[0]):
        out_ref[k] = refs[k][...]


def stack(blocks, after=()):
    inside = pl.BlockSpec(memory_space=pltpu.VMEM)
    n = len(blocks)
    return pl.pallas_call(
        stack_kernel,
        out_shape=jax.ShapeDtypeStruct((n, PACK, D), jnp.bfloat16),
        in_specs=[inside] * (n + len(after)),
        out_specs=inside,
        compiler_params=pltpu.CompilerParams(vmem_limit_bytes=8 * 1024 * 1024),
        name="stack_blocks",
        cost_estimate=pl.CostEstimate(flops=0, bytes_accessed=4 * n * PACK * D, transcendentals=0),
    )(*blocks, *after)


def extra_of(ref):
    return ref[ROWS:PACK, 0:256].astype(jnp.float32)[:, :ROWS]


def gate_kernel(*refs):
    refs[-1][...] = refs[0][...]


def gate(value, *others):
    inside = pl.BlockSpec(memory_space=pltpu.VMEM)
    return pl.pallas_call(
        gate_kernel,
        out_shape=jax.ShapeDtypeStruct(value.shape, value.dtype),
        in_specs=[inside] * (1 + len(others)),
        out_specs=inside,
        compiler_params=pltpu.CompilerParams(vmem_limit_bytes=8 * 1024 * 1024),
        name="gate",
        cost_estimate=pl.CostEstimate(flops=0, bytes_accessed=4 * PACK * D, transcendentals=0),
    )(value, *others)


def lay_out(near, left_ref, rank_ref, valid_ref):
    for s in range(2 * NEAR):
        left_ref[s * ROWS:(s + 1) * ROWS, :] = near[s][0:ROWS, :]
    extras = [extra_of(ref) for ref in near]
    same = [extra[3:4] == extras[0][3:4] for extra in extras]
    near_rank = jnp.concatenate([jnp.where(same[s], ranks(extras[s]), FAR) for s in range(2 * NEAR)], axis=1)
    rank_ref[...] = jnp.transpose(jnp.broadcast_to(near_rank, (128, LEFT)), (1, 0))
    for s in range(2, 2 * NEAR):
        valid_ref[s - 2] = same[s].astype(jnp.float32)


def panel_maxima(panel, right, left_ref, rank_ref):
    blocks = len(panel)
    width = blocks * ROWS
    for k in range(blocks):
        right[k * ROWS:(k + 1) * ROWS, :] = panel[k][0:ROWS, :]
    panel_rank = jnp.concatenate([ranks(extra_of(ref)) for ref in panel], axis=1)
    split = 2 * ROWS
    cols = []
    rows = None
    for start in range(0, width, TILE):
        tile = min(TILE, width - start)
        sims = lax.dot_general(
            left_ref[...], right[start:start + tile, :], (((1,), (1,)), ((), ())),
            preferred_element_type=jnp.float32,
        )
        for lane in range(0, tile, 128):
            part = sims[:, lane:lane + 128]
            rank_row = panel_rank[:, start + lane:start + lane + 128]
            here = part[:split]
            best = jnp.max(jnp.where(rank_ref[:split] < rank_row, here, -1.0), axis=0, keepdims=True)
            there = part[split:]
            earlier = rank_row < rank_ref[split:]
            best = jnp.maximum(best, jnp.max(jnp.where(earlier, -1.0, there), axis=0, keepdims=True))
            cols.append(best)
            found = jnp.where(earlier, there, -1.0)
            rows = found if rows is None else jnp.maximum(rows, found)
    return jnp.concatenate(cols, axis=1), rows


def first_kernel(place_ref, *refs):
    *given, cols_ref, rows_ref, left_ref, rank_ref, valid_ref, right = refs
    panel, given = given[:FIRST], given[FIRST:]
    mine, theirs = given[:len(given) // 2], given[len(given) // 2:]
    near = []
    for pair in zip(mine, theirs):
        if len(pair[0].shape) == 2:
            near += pair
        else:
            near += [ref.at[k] for k in range(pair[0].shape[0]) for ref in pair]
    lay_out(near, left_ref, rank_ref, valid_ref)
    best, rows = panel_maxima(panel, right, left_ref, rank_ref)
    cols_ref[...] = jnp.full(cols_ref.shape, -1.0, jnp.float32)
    for k in range(FIRST):
        cols_ref[place_ref[k]] = best[:, k * ROWS:(k + 1) * ROWS]
    rows_ref[...] = rows


def last_kernel(place_ref, *refs):
    *given, cols_in_ref, rows_in_ref, left_ref, rank_ref, valid_ref, cols_ref, mine_ref, theirs_ref, right = refs
    panel = [ref.at[k] for ref in given for k in range(2)] if len(given) == 1 else given
    best, rows = panel_maxima(panel, right, left_ref, rank_ref)
    cols_ref[...] = cols_in_ref[...]
    for k in range(2 * X - FIRST):
        cols_ref[place_ref[FIRST + k]] = best[:, k * ROWS:(k + 1) * ROWS]
    rows = jnp.maximum(rows, rows_in_ref[...])
    line = jnp.max(jnp.transpose(rows, (1, 0)), axis=0, keepdims=True)
    for s in range(NEAR - 1):
        for k, ref in enumerate((mine_ref, theirs_ref)):
            at = 2 * s + k
            ref[s] = jnp.where(valid_ref[at] > 0.5, line[:, at * ROWS:(at + 1) * ROWS], -1.0)


def cost(blocks):
    return pl.CostEstimate(
        flops=2 * LEFT * blocks * ROWS * D, bytes_accessed=2 * (2 * NEAR + blocks) * PACK * D, transcendentals=0
    )


def first_maxima(place, near, panel):
    inside = pl.BlockSpec(memory_space=pltpu.VMEM)
    blocks = len(panel)
    return pl.pallas_call(
        first_kernel,
        out_shape=(
            jax.ShapeDtypeStruct((2 * X, 1, ROWS), jnp.float32),
            jax.ShapeDtypeStruct((LEFT - 2 * ROWS, 128), jnp.float32),
            jax.ShapeDtypeStruct((LEFT, D), jnp.bfloat16),
            jax.ShapeDtypeStruct((LEFT, 128), jnp.float32),
            jax.ShapeDtypeStruct((2 * (NEAR - 1), 1, ROWS), jnp.float32),
        ),
        in_specs=[pl.BlockSpec(memory_space=pltpu.SMEM)] + [inside] * (len(near) + blocks),
        out_specs=(inside,) * 5,
        scratch_shapes=[pltpu.VMEM((blocks * ROWS, D), jnp.bfloat16)],
        compiler_params=pltpu.CompilerParams(vmem_limit_bytes=20 * 1024 * 1024),
        name="first_maxima",
        cost_estimate=cost(blocks),
    )(place, *panel, *near)


def last_maxima(place, panel, carried):
    inside = pl.BlockSpec(memory_space=pltpu.VMEM)
    lines = jax.ShapeDtypeStruct((NEAR - 1, 1, ROWS), jnp.float32)
    blocks = 2 * X - FIRST
    return pl.pallas_call(
        last_kernel,
        out_shape=(jax.ShapeDtypeStruct((2 * X, 1, ROWS), jnp.float32), lines, lines),
        in_specs=[pl.BlockSpec(memory_space=pltpu.SMEM)] + [inside] * (len(panel) + len(carried)),
        out_specs=(inside,) * 3,
        scratch_shapes=[pltpu.VMEM((blocks * ROWS, D), jnp.bfloat16)],
        compiler_params=pltpu.CompilerParams(vmem_limit_bytes=20 * 1024 * 1024),
        name="last_maxima",
        cost_estimate=cost(blocks),
    )(place, *panel, *carried)


def half_flip(value, count):
    pairs = []
    for g in range(count):
        low, y = divmod(g, count // Z_LO)
        for h in range(2):
            for c in range(2):
                z = (h * Z_LO + low + (2 if c == 0 else 2 * Z_LO - 2)) % (2 * Z_LO)
                target = z % Z_LO * (count // Z_LO) + y
                pairs.append(((g * 2 + h) * 2 + c, (target * 2 + z // Z_LO) * 2 + c))
    return lax.ppermute(value, ("grp", "zh", "core"), pairs)


def shift(value, steps, count):
    pairs = [(i, i + steps) for i in range(count) if 0 <= i + steps < count]
    return lax.ppermute(value, "grp", pairs)


def swap(value, axis):
    return lax.ppermute(value, axis, [(0, 1), (1, 0)])


def turn_x(value, even):
    pairs = [(2 * i, 2 * ((i + even) % X)) for i in range(X)]
    pairs += [(2 * i + 1, 2 * ((i + X - even) % X) + 1) for i in range(X)]
    return lax.ppermute(value, ("x", "core"), pairs)


def per_device(embeddings, labels, order):
    count = lax.axis_size("grp")
    grp, zh, x, core = (lax.axis_index(axis) for axis in ("grp", "zh", "x", "core"))
    block = pack(embeddings, labels, order)
    one = shift(block, MOVES[0], count)
    two = shift(block, MOVES[1], count)
    three = shift(block, MOVES[2], count)
    ahead, behind = turn_x(block, 1), turn_x(block, -1)
    across = turn_x(ahead, 1)
    sib = swap(block, "core")
    flipped = gate(swap(block, "zh"), ahead)
    flip_ahead = turn_x(flipped, 1)
    flip_behind = turn_x(gate(flipped, across, behind), -1)
    flip_across = turn_x(flip_ahead, 1)
    mine = (block, one, stack((two, three)))
    theirs = [sib] + [swap(value, "core") for value in mine[1:]]
    turn = jnp.where(core == 0, 1, X - 1)
    order_held = ((0, 0), (1, 0), (0, 1), (1, 1), (0, X - 1), (0, 2), (1, X - 1), (1, 2))
    slots = [(zh + h) % 2 * X + (x + (X - k) * turn) % X for h, k in order_held]
    place = jnp.stack(slots).astype(jnp.int32)
    carried = first_maxima(place, (*mine, *theirs), [block, flipped, ahead, flip_ahead, behind, across])
    cols, rows, rows_sib = last_maxima(place, [flip_behind, flip_across], carried)
    best = jnp.max(lax.all_to_all(cols, ("zh", "x"), 0, 0, tiled=True), axis=0)
    mine = jnp.maximum(rows, swap(rows_sib, "core"))
    for i, steps in enumerate(MOVES):
        back = shift(mine[i], -steps, count)
        source = grp + steps
        best = jnp.maximum(best, jnp.where((source >= 0) & (source < count), back, -1.0))
    return best.reshape(ROWS)


def solution(mesh):
    axes = ("grp", "zh", "x", "core")
    fine = Mesh(mesh.devices.reshape(mesh.shape["grp"], 2, X, 2), axes)
    return jax.shard_map(
        per_device,
        mesh=fine,
        in_specs=(P(axes, None), P(axes), P(axes)),
        out_specs=P(axes),
        check_vma=False,
    )
```

```python
import jax
import jax.numpy as jnp
from jax import lax
from jax.experimental import pallas as pl
from jax.experimental.pallas import tpu as pltpu
from jax.sharding import Mesh, PartitionSpec as P

ROWS = 192
EXTRA = 8
PACK = ROWS + EXTRA
D = 1024
X = 4
MOVES = (1, -3, 2)
NEAR = 1 + len(MOVES)
LEFT = 2 * NEAR * ROWS
TILE = 256
FAR = 1.0e9
FIRST = 6
HELD = ((0, 0), (1, 0), (0, 1), (1, 1), (0, 3), (0, 2), (1, 3), (1, 2))


def pack_kernel(emb_any, lab_any, ord_any, out_ref, emb_ref, lab_ref, ord_ref, sems):
    copies = [
        pltpu.make_async_copy(source, target, sems.at[k])
        for k, (source, target) in enumerate(((emb_any, emb_ref), (lab_any, lab_ref), (ord_any, ord_ref)))
    ]
    for copy in copies:
        copy.start()
    for copy in copies:
        copy.wait()
    values = emb_ref[...].astype(jnp.float32)
    scale = lax.rsqrt(jnp.sum(values * values, axis=1, keepdims=True) + 1e-06)
    out_ref[0:ROWS, :] = (values * scale).astype(jnp.bfloat16)
    rank = jnp.broadcast_to(ord_ref[...], (EXTRA, ROWS))
    label = jnp.broadcast_to(lab_ref[...], (EXTRA, ROWS))
    line = lax.broadcasted_iota(jnp.int32, (EXTRA, ROWS), 0)
    digits = jnp.where(
        line == 0,
        rank >> 12,
        jnp.where(line == 1, (rank >> 6) & 63, jnp.where(line == 2, rank & 63, label + 1)),
    )
    digits = jnp.where(line < 4, digits, 0).astype(jnp.float32)
    digits = jnp.concatenate([digits, jnp.zeros((EXTRA, D - ROWS), jnp.float32)], axis=1)
    out_ref[ROWS:PACK, :] = digits.astype(jnp.bfloat16)


def pack(embeddings, labels, order):
    anywhere = pl.BlockSpec(memory_space=pl.ANY)
    return pl.pallas_call(
        pack_kernel,
        out_shape=jax.ShapeDtypeStruct((PACK, D), jnp.bfloat16),
        in_specs=[anywhere] * 3,
        out_specs=pl.BlockSpec(memory_space=pltpu.VMEM),
        scratch_shapes=[
            pltpu.VMEM((ROWS, D), jnp.bfloat16),
            pltpu.VMEM((1, ROWS), jnp.int32),
            pltpu.VMEM((1, ROWS), jnp.int32),
            pltpu.SemaphoreType.DMA((3,)),
        ],
        name="normalize_pack",
        cost_estimate=pl.CostEstimate(flops=4 * ROWS * D, bytes_accessed=4 * ROWS * D, transcendentals=ROWS),
    )(embeddings, labels.reshape(1, ROWS), order.reshape(1, ROWS))


def ranks(extra):
    return extra[0:1] * 4096.0 + extra[1:2] * 64.0 + extra[2:3]


def stack_kernel(*refs):
    out_ref = refs[-1]
    for k in range(out_ref.shape[0]):
        out_ref[k] = refs[k][...]


def stack(blocks, after=()):
    inside = pl.BlockSpec(memory_space=pltpu.VMEM)
    n = len(blocks)
    return pl.pallas_call(
        stack_kernel,
        out_shape=jax.ShapeDtypeStruct((n, PACK, D), jnp.bfloat16),
        in_specs=[inside] * (n + len(after)),
        out_specs=inside,
        compiler_params=pltpu.CompilerParams(vmem_limit_bytes=8 * 1024 * 1024),
        name="stack_blocks",
        cost_estimate=pl.CostEstimate(flops=0, bytes_accessed=4 * n * PACK * D, transcendentals=0),
    )(*blocks, *after)


def extra_of(ref):
    return ref[ROWS:PACK, 0:256].astype(jnp.float32)[:, :ROWS]


def gate_kernel(*refs):
    refs[-1][...] = refs[0][...]


def gate(value, *others):
    inside = pl.BlockSpec(memory_space=pltpu.VMEM)
    return pl.pallas_call(
        gate_kernel,
        out_shape=jax.ShapeDtypeStruct(value.shape, value.dtype),
        in_specs=[inside] * (1 + len(others)),
        out_specs=inside,
        compiler_params=pltpu.CompilerParams(vmem_limit_bytes=8 * 1024 * 1024),
        name="gate",
        cost_estimate=pl.CostEstimate(flops=0, bytes_accessed=4 * PACK * D, transcendentals=0),
    )(value, *others)


def lay_out(near, left_ref, rank_ref, valid_ref):
    for s in range(2 * NEAR):
        left_ref[s * ROWS:(s + 1) * ROWS, :] = near[s][0:ROWS, :]
    extras = [extra_of(ref) for ref in near]
    same = [extra[3:4] == extras[0][3:4] for extra in extras]
    near_rank = jnp.concatenate([jnp.where(same[s], ranks(extras[s]), FAR) for s in range(2 * NEAR)], axis=1)
    rank_ref[...] = jnp.transpose(jnp.broadcast_to(near_rank, (128, LEFT)), (1, 0))
    for s in range(2, 2 * NEAR):
        valid_ref[s - 2] = same[s].astype(jnp.float32)


def panel_maxima(panel, right, left_ref, rank_ref):
    blocks = len(panel)
    width = blocks * ROWS
    for k in range(blocks):
        right[k * ROWS:(k + 1) * ROWS, :] = panel[k][0:ROWS, :]
    panel_rank = jnp.concatenate([ranks(extra_of(ref)) for ref in panel], axis=1)
    split = 2 * ROWS
    cols = []
    rows = None
    for start in range(0, width, TILE):
        tile = min(TILE, width - start)
        sims = lax.dot_general(
            left_ref[...], right[start:start + tile, :], (((1,), (1,)), ((), ())),
            preferred_element_type=jnp.float32,
        )
        for lane in range(0, tile, 128):
            part = sims[:, lane:lane + 128]
            rank_row = panel_rank[:, start + lane:start + lane + 128]
            here = part[:split]
            best = jnp.max(jnp.where(rank_ref[:split] < rank_row, here, -1.0), axis=0, keepdims=True)
            there = part[split:]
            earlier = rank_row < rank_ref[split:]
            best = jnp.maximum(best, jnp.max(jnp.where(earlier, -1.0, there), axis=0, keepdims=True))
            cols.append(best)
            found = jnp.where(earlier, there, -1.0)
            rows = found if rows is None else jnp.maximum(rows, found)
    return jnp.concatenate(cols, axis=1), rows


def slot(number):
    zh, x, core = (lax.axis_index(axis) for axis in ("zh", "x", "core"))
    half, step = HELD[number]
    turn = jnp.where(core == 0, X - step, step)
    return lax.rem(zh + half, 2) * X + lax.rem(x + turn, X)


def first_kernel(*refs):
    *given, cols_ref, rows_ref, left_ref, rank_ref, valid_ref, right = refs
    panel, given = given[:FIRST], given[FIRST:]
    mine, theirs = given[:len(given) // 2], given[len(given) // 2:]
    near = []
    for pair in zip(mine, theirs):
        if len(pair[0].shape) == 2:
            near += pair
        else:
            near += [ref.at[k] for k in range(pair[0].shape[0]) for ref in pair]
    lay_out(near, left_ref, rank_ref, valid_ref)
    best, rows = panel_maxima(panel, right, left_ref, rank_ref)
    cols_ref[...] = jnp.full(cols_ref.shape, -1.0, jnp.float32)
    for k in range(FIRST):
        cols_ref[slot(k)] = best[:, k * ROWS:(k + 1) * ROWS]
    rows_ref[...] = rows


def last_kernel(*refs):
    *given, cols_in_ref, rows_in_ref, left_ref, rank_ref, valid_ref, cols_ref, mine_ref, theirs_ref, right = refs
    panel = [ref.at[k] for ref in given for k in range(2)] if len(given) == 1 else given
    best, rows = panel_maxima(panel, right, left_ref, rank_ref)
    cols_ref[...] = cols_in_ref[...]
    for k in range(2 * X - FIRST):
        cols_ref[slot(FIRST + k)] = best[:, k * ROWS:(k + 1) * ROWS]
    rows = jnp.maximum(rows, rows_in_ref[...])
    line = jnp.max(jnp.transpose(rows, (1, 0)), axis=0, keepdims=True)
    for s in range(NEAR - 1):
        for k, ref in enumerate((mine_ref, theirs_ref)):
            at = 2 * s + k
            ref[s] = jnp.where(valid_ref[at] > 0.5, line[:, at * ROWS:(at + 1) * ROWS], -1.0)


def cost(blocks):
    return pl.CostEstimate(
        flops=2 * LEFT * blocks * ROWS * D, bytes_accessed=2 * (2 * NEAR + blocks) * PACK * D, transcendentals=0
    )


def first_maxima(near, panel):
    inside = pl.BlockSpec(memory_space=pltpu.VMEM)
    blocks = len(panel)
    return pl.pallas_call(
        first_kernel,
        out_shape=(
            jax.ShapeDtypeStruct((2 * X, 1, ROWS), jnp.float32),
            jax.ShapeDtypeStruct((LEFT - 2 * ROWS, 128), jnp.float32),
            jax.ShapeDtypeStruct((LEFT, D), jnp.bfloat16),
            jax.ShapeDtypeStruct((LEFT, 128), jnp.float32),
            jax.ShapeDtypeStruct((2 * (NEAR - 1), 1, ROWS), jnp.float32),
        ),
        in_specs=[inside] * (len(near) + blocks),
        out_specs=(inside,) * 5,
        scratch_shapes=[pltpu.VMEM((blocks * ROWS, D), jnp.bfloat16)],
        compiler_params=pltpu.CompilerParams(vmem_limit_bytes=20 * 1024 * 1024),
        name="first_maxima",
        cost_estimate=cost(blocks),
    )(*panel, *near)


def last_maxima(panel, carried):
    inside = pl.BlockSpec(memory_space=pltpu.VMEM)
    lines = jax.ShapeDtypeStruct((NEAR - 1, 1, ROWS), jnp.float32)
    blocks = 2 * X - FIRST
    return pl.pallas_call(
        last_kernel,
        out_shape=(jax.ShapeDtypeStruct((2 * X, 1, ROWS), jnp.float32), lines, lines),
        in_specs=[inside] * (len(panel) + len(carried)),
        out_specs=(inside,) * 3,
        scratch_shapes=[pltpu.VMEM((blocks * ROWS, D), jnp.bfloat16)],
        compiler_params=pltpu.CompilerParams(vmem_limit_bytes=20 * 1024 * 1024),
        name="last_maxima",
        cost_estimate=cost(blocks),
    )(*panel, *carried)


def shift(value, steps, count):
    pairs = [(i, i + steps) for i in range(count) if 0 <= i + steps < count]
    return lax.ppermute(value, "grp", pairs)


def swap(value, axis):
    return lax.ppermute(value, axis, [(0, 1), (1, 0)])


def turn_x(value, even):
    pairs = [(2 * i, 2 * ((i + even) % X)) for i in range(X)]
    pairs += [(2 * i + 1, 2 * ((i + X - even) % X) + 1) for i in range(X)]
    return lax.ppermute(value, ("x", "core"), pairs)


def per_device(embeddings, labels, order):
    count = lax.axis_size("grp")
    grp = lax.axis_index("grp")
    block = pack(embeddings, labels, order)
    one, far, two = (shift(block, steps, count) for steps in MOVES)
    ahead, behind = turn_x(block, 1), turn_x(block, -1)
    across = turn_x(ahead, 1)
    sib = swap(block, "core")
    flipped = gate(swap(block, "zh"), ahead)
    flip_ahead = turn_x(flipped, 1)
    flip_behind = turn_x(gate(flipped, across, behind), -1)
    flip_across = turn_x(flip_ahead, 1)
    mine = (block, stack((one, far)), two)
    theirs = [swap(value, "core") for value in mine]
    carried = first_maxima((*mine, *theirs), [block, flipped, ahead, flip_ahead, behind, across])
    cols, rows, rows_sib = last_maxima([flip_behind, flip_across], carried)
    best = jnp.max(lax.all_to_all(cols, ("zh", "x"), 0, 0, tiled=True), axis=0)
    mine = jnp.maximum(rows, swap(rows_sib, "core"))
    for i, steps in enumerate(MOVES):
        back = shift(mine[i], -steps, count)
        source = grp + steps
        best = jnp.maximum(best, jnp.where((source >= 0) & (source < count), back, -1.0))
    return best.reshape(ROWS)


def solution(mesh):
    axes = ("grp", "zh", "x", "core")
    fine = Mesh(mesh.devices.reshape(mesh.shape["grp"], 2, X, 2), axes)
    return jax.shard_map(
        per_device,
        mesh=fine,
        in_specs=(P(axes, None), P(axes), P(axes)),
        out_specs=P(axes),
        check_vma=False,
    )
```

```python
import jax
import jax.numpy as jnp
from jax import lax
from jax.experimental import pallas as pl
from jax.experimental.pallas import tpu as pltpu
from jax.sharding import Mesh, PartitionSpec as P

ROWS = 192
EXTRA = 8
PAD = 8
PACK = ROWS + EXTRA
D = 1024
X = 4
MOVES = (1, -3, 2)
NEAR = 1 + len(MOVES)
LEFT = 2 * NEAR * ROWS
TILE = 256
FAR = 1.0e9
FIRST = 6
HELD = ((0, 0), (1, 0), (0, 1), (1, 1), (0, 3), (0, 2), (1, 3), (1, 2))


def pack_kernel(emb_any, lab_any, ord_any, out_ref, tall_ref, emb_ref, lab_ref, ord_ref, sems):
    copies = [
        pltpu.make_async_copy(source, target, sems.at[k])
        for k, (source, target) in enumerate(((emb_any, emb_ref), (lab_any, lab_ref), (ord_any, ord_ref)))
    ]
    for copy in copies:
        copy.start()
    for copy in copies:
        copy.wait()
    values = emb_ref[...].astype(jnp.float32)
    scale = lax.rsqrt(jnp.sum(values * values, axis=1, keepdims=True) + 1e-06)
    out_ref[0:ROWS, :] = (values * scale).astype(jnp.bfloat16)
    rank = jnp.broadcast_to(ord_ref[...], (EXTRA, ROWS))
    label = jnp.broadcast_to(lab_ref[...], (EXTRA, ROWS))
    line = lax.broadcasted_iota(jnp.int32, (EXTRA, ROWS), 0)
    digits = jnp.where(
        line == 0,
        rank >> 12,
        jnp.where(line == 1, (rank >> 6) & 63, jnp.where(line == 2, rank & 63, label + 1)),
    )
    digits = jnp.where(line < 4, digits, 0).astype(jnp.float32)
    digits = jnp.concatenate([digits, jnp.zeros((EXTRA, D - ROWS), jnp.float32)], axis=1)
    out_ref[ROWS:PACK, :] = digits.astype(jnp.bfloat16)
    tall_ref[0:PACK, :] = out_ref[...]
    tall_ref[PACK:PACK + PAD, :] = jnp.zeros((PAD, D), jnp.bfloat16)


def pack(embeddings, labels, order):
    anywhere = pl.BlockSpec(memory_space=pl.ANY)
    return pl.pallas_call(
        pack_kernel,
        out_shape=(
            jax.ShapeDtypeStruct((PACK, D), jnp.bfloat16),
            jax.ShapeDtypeStruct((PACK + PAD, D), jnp.bfloat16),
        ),
        in_specs=[anywhere] * 3,
        out_specs=(pl.BlockSpec(memory_space=pltpu.VMEM),) * 2,
        scratch_shapes=[
            pltpu.VMEM((ROWS, D), jnp.bfloat16),
            pltpu.VMEM((1, ROWS), jnp.int32),
            pltpu.VMEM((1, ROWS), jnp.int32),
            pltpu.SemaphoreType.DMA((3,)),
        ],
        name="normalize_pack",
        cost_estimate=pl.CostEstimate(flops=4 * ROWS * D, bytes_accessed=4 * ROWS * D, transcendentals=ROWS),
    )(embeddings, labels.reshape(1, ROWS), order.reshape(1, ROWS))


def ranks(extra):
    return extra[0:1] * 4096.0 + extra[1:2] * 64.0 + extra[2:3]


def stack_kernel(*refs):
    out_ref = refs[-1]
    for k in range(out_ref.shape[0]):
        out_ref[k] = refs[k][...]


def stack(blocks, after=()):
    inside = pl.BlockSpec(memory_space=pltpu.VMEM)
    n = len(blocks)
    return pl.pallas_call(
        stack_kernel,
        out_shape=jax.ShapeDtypeStruct((n, PACK, D), jnp.bfloat16),
        in_specs=[inside] * (n + len(after)),
        out_specs=inside,
        compiler_params=pltpu.CompilerParams(vmem_limit_bytes=8 * 1024 * 1024),
        name="stack_blocks",
        cost_estimate=pl.CostEstimate(flops=0, bytes_accessed=4 * n * PACK * D, transcendentals=0),
    )(*blocks, *after)


def extra_of(ref):
    return ref[ROWS:PACK, 0:256].astype(jnp.float32)[:, :ROWS]


def gate_kernel(*refs):
    refs[-1][...] = refs[0][0:PACK, :]


def gate(value, *others):
    inside = pl.BlockSpec(memory_space=pltpu.VMEM)
    return pl.pallas_call(
        gate_kernel,
        out_shape=jax.ShapeDtypeStruct((PACK, D), value.dtype),
        in_specs=[inside] * (1 + len(others)),
        out_specs=inside,
        compiler_params=pltpu.CompilerParams(vmem_limit_bytes=8 * 1024 * 1024),
        name="gate",
        cost_estimate=pl.CostEstimate(flops=0, bytes_accessed=4 * PACK * D, transcendentals=0),
    )(value, *others)


def lay_out(near, left_ref, rank_ref, valid_ref):
    for s in range(2 * NEAR):
        left_ref[s * ROWS:(s + 1) * ROWS, :] = near[s][0:ROWS, :]
    extras = [extra_of(ref) for ref in near]
    same = [extra[3:4] == extras[0][3:4] for extra in extras]
    near_rank = jnp.concatenate([jnp.where(same[s], ranks(extras[s]), FAR) for s in range(2 * NEAR)], axis=1)
    rank_ref[...] = jnp.transpose(jnp.broadcast_to(near_rank, (128, LEFT)), (1, 0))
    for s in range(2, 2 * NEAR):
        valid_ref[s - 2] = same[s].astype(jnp.float32)


def panel_maxima(panel, right, left_ref, rank_ref):
    blocks = len(panel)
    width = blocks * ROWS
    for k in range(blocks):
        right[k * ROWS:(k + 1) * ROWS, :] = panel[k][0:ROWS, :]
    panel_rank = jnp.concatenate([ranks(extra_of(ref)) for ref in panel], axis=1)
    split = 2 * ROWS
    cols = []
    rows = None
    for start in range(0, width, TILE):
        tile = min(TILE, width - start)
        sims = lax.dot_general(
            left_ref[...], right[start:start + tile, :], (((1,), (1,)), ((), ())),
            preferred_element_type=jnp.float32,
        )
        for lane in range(0, tile, 128):
            part = sims[:, lane:lane + 128]
            rank_row = panel_rank[:, start + lane:start + lane + 128]
            here = part[:split]
            best = jnp.max(jnp.where(rank_ref[:split] < rank_row, here, -1.0), axis=0, keepdims=True)
            there = part[split:]
            earlier = rank_row < rank_ref[split:]
            best = jnp.maximum(best, jnp.max(jnp.where(earlier, -1.0, there), axis=0, keepdims=True))
            cols.append(best)
            found = jnp.where(earlier, there, -1.0)
            rows = found if rows is None else jnp.maximum(rows, found)
    return jnp.concatenate(cols, axis=1), rows


def slot(number):
    zh, x, core = (lax.axis_index(axis) for axis in ("zh", "x", "core"))
    half, step = HELD[number]
    turn = jnp.where(core == 0, X - step, step)
    return lax.rem(zh + half, 2) * X + lax.rem(x + turn, X)


def first_kernel(*refs):
    *given, cols_ref, rows_ref, left_ref, rank_ref, valid_ref, right = refs
    panel, given = given[:FIRST], given[FIRST:]
    mine, theirs = given[:len(given) // 2], given[len(given) // 2:]
    near = []
    for pair in zip(mine, theirs):
        if len(pair[0].shape) == 2:
            near += pair
        else:
            near += [ref.at[k] for k in range(pair[0].shape[0]) for ref in pair]
    lay_out(near, left_ref, rank_ref, valid_ref)
    best, rows = panel_maxima(panel, right, left_ref, rank_ref)
    cols_ref[...] = jnp.full(cols_ref.shape, -1.0, jnp.float32)
    for k in range(FIRST):
        cols_ref[slot(k)] = best[:, k * ROWS:(k + 1) * ROWS]
    rows_ref[...] = rows


def last_kernel(*refs):
    *given, cols_in_ref, rows_in_ref, left_ref, rank_ref, valid_ref, cols_ref, mine_ref, theirs_ref, right = refs
    panel = [ref.at[k] for ref in given for k in range(2)] if len(given) == 1 else given
    best, rows = panel_maxima(panel, right, left_ref, rank_ref)
    cols_ref[...] = cols_in_ref[...]
    for k in range(2 * X - FIRST):
        cols_ref[slot(FIRST + k)] = best[:, k * ROWS:(k + 1) * ROWS]
    rows = jnp.maximum(rows, rows_in_ref[...])
    line = jnp.max(jnp.transpose(rows, (1, 0)), axis=0, keepdims=True)
    for s in range(NEAR - 1):
        for k, ref in enumerate((mine_ref, theirs_ref)):
            at = 2 * s + k
            ref[s] = jnp.where(valid_ref[at] > 0.5, line[:, at * ROWS:(at + 1) * ROWS], -1.0)


def cost(blocks):
    return pl.CostEstimate(
        flops=2 * LEFT * blocks * ROWS * D, bytes_accessed=2 * (2 * NEAR + blocks) * PACK * D, transcendentals=0
    )


def first_maxima(near, panel):
    inside = pl.BlockSpec(memory_space=pltpu.VMEM)
    blocks = len(panel)
    return pl.pallas_call(
        first_kernel,
        out_shape=(
            jax.ShapeDtypeStruct((2 * X, 1, ROWS), jnp.float32),
            jax.ShapeDtypeStruct((LEFT - 2 * ROWS, 128), jnp.float32),
            jax.ShapeDtypeStruct((LEFT, D), jnp.bfloat16),
            jax.ShapeDtypeStruct((LEFT, 128), jnp.float32),
            jax.ShapeDtypeStruct((2 * (NEAR - 1), 1, ROWS), jnp.float32),
        ),
        in_specs=[inside] * (len(near) + blocks),
        out_specs=(inside,) * 5,
        scratch_shapes=[pltpu.VMEM((blocks * ROWS, D), jnp.bfloat16)],
        compiler_params=pltpu.CompilerParams(vmem_limit_bytes=20 * 1024 * 1024),
        name="first_maxima",
        cost_estimate=cost(blocks),
    )(*panel, *near)


def last_maxima(panel, carried):
    inside = pl.BlockSpec(memory_space=pltpu.VMEM)
    lines = jax.ShapeDtypeStruct((NEAR - 1, 1, ROWS), jnp.float32)
    blocks = 2 * X - FIRST
    return pl.pallas_call(
        last_kernel,
        out_shape=(jax.ShapeDtypeStruct((2 * X, 1, ROWS), jnp.float32), lines, lines),
        in_specs=[inside] * (len(panel) + len(carried)),
        out_specs=(inside,) * 3,
        scratch_shapes=[pltpu.VMEM((blocks * ROWS, D), jnp.bfloat16)],
        compiler_params=pltpu.CompilerParams(vmem_limit_bytes=20 * 1024 * 1024),
        name="last_maxima",
        cost_estimate=cost(blocks),
    )(*panel, *carried)


def shift(value, steps, count):
    pairs = [(i, i + steps) for i in range(count) if 0 <= i + steps < count]
    return lax.ppermute(value, "grp", pairs)


def swap(value, axis):
    return lax.ppermute(value, axis, [(0, 1), (1, 0)])


def turn_x(value, even):
    pairs = [(2 * i, 2 * ((i + even) % X)) for i in range(X)]
    pairs += [(2 * i + 1, 2 * ((i + X - even) % X) + 1) for i in range(X)]
    return lax.ppermute(value, ("x", "core"), pairs)


def per_device(embeddings, labels, order):
    count = lax.axis_size("grp")
    grp = lax.axis_index("grp")
    block, tall = pack(embeddings, labels, order)
    one, far, two = (shift(block, steps, count) for steps in MOVES)
    ahead, behind = turn_x(block, 1), turn_x(block, -1)
    across = turn_x(ahead, 1)
    sib = swap(block, "core")
    flipped = gate(swap(tall, "zh"), ahead)
    flip_ahead = turn_x(flipped, 1)
    flip_behind = turn_x(gate(flipped, across, behind), -1)
    flip_across = turn_x(flip_ahead, 1)
    mine = (block, stack((one, far)), two)
    theirs = [swap(value, "core") for value in mine]
    carried = first_maxima((*mine, *theirs), [block, flipped, ahead, flip_ahead, behind, across])
    cols, rows, rows_sib = last_maxima([flip_behind, flip_across], carried)
    best = jnp.max(lax.all_to_all(cols, ("zh", "x"), 0, 0, tiled=True), axis=0)
    mine = jnp.maximum(rows, swap(rows_sib, "core"))
    for i, steps in enumerate(MOVES):
        back = shift(mine[i], -steps, count)
        source = grp + steps
        best = jnp.maximum(best, jnp.where((source >= 0) & (source < count), back, -1.0))
    return best.reshape(ROWS)


def solution(mesh):
    axes = ("grp", "zh", "x", "core")
    fine = Mesh(mesh.devices.reshape(mesh.shape["grp"], 2, X, 2), axes)
    return jax.shard_map(
        per_device,
        mesh=fine,
        in_specs=(P(axes, None), P(axes), P(axes)),
        out_specs=P(axes),
        check_vma=False,
    )
```

```python
import jax
import jax.numpy as jnp
from jax import lax
from jax.experimental import pallas as pl
from jax.experimental.pallas import tpu as pltpu
from jax.sharding import Mesh, PartitionSpec as P

ROWS = 192
EXTRA = 8
PAD = 8
PACK = ROWS + EXTRA
D = 1024
X = 4
MOVES = (1, -3, 2)
NEAR = 1 + len(MOVES)
LEFT = 2 * NEAR * ROWS
TILE = 256
FAR = 1.0e9
FIRST = 6
HELD = ((0, 0), (1, 0), (0, 1), (1, 1), (0, 3), (1, 3), (0, 2), (1, 2))


def pack_kernel(emb_any, lab_any, ord_any, out_ref, tall_ref, emb_ref, lab_ref, ord_ref, sems):
    copies = [
        pltpu.make_async_copy(source, target, sems.at[k])
        for k, (source, target) in enumerate(((emb_any, emb_ref), (lab_any, lab_ref), (ord_any, ord_ref)))
    ]
    for copy in copies:
        copy.start()
    for copy in copies:
        copy.wait()
    values = emb_ref[...].astype(jnp.float32)
    scale = lax.rsqrt(jnp.sum(values * values, axis=1, keepdims=True) + 1e-06)
    out_ref[0:ROWS, :] = (values * scale).astype(jnp.bfloat16)
    rank = jnp.broadcast_to(ord_ref[...], (EXTRA, ROWS))
    label = jnp.broadcast_to(lab_ref[...], (EXTRA, ROWS))
    line = lax.broadcasted_iota(jnp.int32, (EXTRA, ROWS), 0)
    digits = jnp.where(
        line == 0,
        rank >> 12,
        jnp.where(line == 1, (rank >> 6) & 63, jnp.where(line == 2, rank & 63, label + 1)),
    )
    digits = jnp.where(line < 4, digits, 0).astype(jnp.float32)
    digits = jnp.concatenate([digits, jnp.zeros((EXTRA, D - ROWS), jnp.float32)], axis=1)
    out_ref[ROWS:PACK, :] = digits.astype(jnp.bfloat16)
    tall_ref[0:PACK, :] = out_ref[...]
    tall_ref[PACK:PACK + PAD, :] = jnp.zeros((PAD, D), jnp.bfloat16)


def pack(embeddings, labels, order):
    anywhere = pl.BlockSpec(memory_space=pl.ANY)
    return pl.pallas_call(
        pack_kernel,
        out_shape=(
            jax.ShapeDtypeStruct((PACK, D), jnp.bfloat16),
            jax.ShapeDtypeStruct((PACK + PAD, D), jnp.bfloat16),
        ),
        in_specs=[anywhere] * 3,
        out_specs=(pl.BlockSpec(memory_space=pltpu.VMEM),) * 2,
        scratch_shapes=[
            pltpu.VMEM((ROWS, D), jnp.bfloat16),
            pltpu.VMEM((1, ROWS), jnp.int32),
            pltpu.VMEM((1, ROWS), jnp.int32),
            pltpu.SemaphoreType.DMA((3,)),
        ],
        name="normalize_pack",
        cost_estimate=pl.CostEstimate(flops=4 * ROWS * D, bytes_accessed=4 * ROWS * D, transcendentals=ROWS),
    )(embeddings, labels.reshape(1, ROWS), order.reshape(1, ROWS))


def ranks(extra):
    return extra[0:1] * 4096.0 + extra[1:2] * 64.0 + extra[2:3]


def stack_kernel(*refs):
    out_ref = refs[-1]
    for k in range(out_ref.shape[0]):
        out_ref[k] = refs[k][...]


def stack(blocks, after=()):
    inside = pl.BlockSpec(memory_space=pltpu.VMEM)
    n = len(blocks)
    return pl.pallas_call(
        stack_kernel,
        out_shape=jax.ShapeDtypeStruct((n, PACK, D), jnp.bfloat16),
        in_specs=[inside] * (n + len(after)),
        out_specs=inside,
        compiler_params=pltpu.CompilerParams(vmem_limit_bytes=8 * 1024 * 1024),
        name="stack_blocks",
        cost_estimate=pl.CostEstimate(flops=0, bytes_accessed=4 * n * PACK * D, transcendentals=0),
    )(*blocks, *after)


def extra_of(ref):
    return ref[ROWS:PACK, 0:256].astype(jnp.float32)[:, :ROWS]


def gate_kernel(*refs):
    refs[-1][...] = refs[0][0:PACK, :]


def gate(value, *others):
    inside = pl.BlockSpec(memory_space=pltpu.VMEM)
    return pl.pallas_call(
        gate_kernel,
        out_shape=jax.ShapeDtypeStruct((PACK, D), value.dtype),
        in_specs=[inside] * (1 + len(others)),
        out_specs=inside,
        compiler_params=pltpu.CompilerParams(vmem_limit_bytes=8 * 1024 * 1024),
        name="gate",
        cost_estimate=pl.CostEstimate(flops=0, bytes_accessed=4 * PACK * D, transcendentals=0),
    )(value, *others)


def lay_out(near, left_ref, rank_ref, valid_ref):
    for s in range(2 * NEAR):
        left_ref[s * ROWS:(s + 1) * ROWS, :] = near[s][0:ROWS, :]
    extras = [extra_of(ref) for ref in near]
    same = [extra[3:4] == extras[0][3:4] for extra in extras]
    near_rank = jnp.concatenate([jnp.where(same[s], ranks(extras[s]), FAR) for s in range(2 * NEAR)], axis=1)
    rank_ref[...] = jnp.transpose(jnp.broadcast_to(near_rank, (128, LEFT)), (1, 0))
    for s in range(2, 2 * NEAR):
        valid_ref[s - 2] = same[s].astype(jnp.float32)


def panel_maxima(panel, right, left_ref, rank_ref):
    blocks = len(panel)
    width = blocks * ROWS
    for k in range(blocks):
        right[k * ROWS:(k + 1) * ROWS, :] = panel[k][0:ROWS, :]
    panel_rank = jnp.concatenate([ranks(extra_of(ref)) for ref in panel], axis=1)
    split = 2 * ROWS
    cols = []
    rows = None
    for start in range(0, width, TILE):
        tile = min(TILE, width - start)
        sims = lax.dot_general(
            left_ref[...], right[start:start + tile, :], (((1,), (1,)), ((), ())),
            preferred_element_type=jnp.float32,
        )
        for lane in range(0, tile, 128):
            part = sims[:, lane:lane + 128]
            rank_row = panel_rank[:, start + lane:start + lane + 128]
            here = part[:split]
            best = jnp.max(jnp.where(rank_ref[:split] < rank_row, here, -1.0), axis=0, keepdims=True)
            there = part[split:]
            earlier = rank_row < rank_ref[split:]
            best = jnp.maximum(best, jnp.max(jnp.where(earlier, -1.0, there), axis=0, keepdims=True))
            cols.append(best)
            found = jnp.where(earlier, there, -1.0)
            rows = found if rows is None else jnp.maximum(rows, found)
    return jnp.concatenate(cols, axis=1), rows


def slot(number):
    zh, x, core = (lax.axis_index(axis) for axis in ("zh", "x", "core"))
    half, step = HELD[number]
    turn = jnp.where(core == 0, X - step, step)
    return lax.rem(zh + half, 2) * X + lax.rem(x + turn, X)


def first_kernel(*refs):
    *given, cols_ref, rows_ref, left_ref, rank_ref, valid_ref, right = refs
    panel, given = given[:FIRST], given[FIRST:]
    mine, theirs = given[:len(given) // 2], given[len(given) // 2:]
    near = []
    for pair in zip(mine, theirs):
        if len(pair[0].shape) == 2:
            near += pair
        else:
            near += [ref.at[k] for k in range(pair[0].shape[0]) for ref in pair]
    lay_out(near, left_ref, rank_ref, valid_ref)
    best, rows = panel_maxima(panel, right, left_ref, rank_ref)
    cols_ref[...] = jnp.full(cols_ref.shape, -1.0, jnp.float32)
    for k in range(FIRST):
        cols_ref[slot(k)] = best[:, k * ROWS:(k + 1) * ROWS]
    rows_ref[...] = rows


def last_kernel(*refs):
    *given, cols_in_ref, rows_in_ref, left_ref, rank_ref, valid_ref, cols_ref, mine_ref, theirs_ref, right = refs
    panel = [ref.at[k] for ref in given for k in range(2)] if len(given) == 1 else given
    best, rows = panel_maxima(panel, right, left_ref, rank_ref)
    cols_ref[...] = cols_in_ref[...]
    for k in range(2 * X - FIRST):
        cols_ref[slot(FIRST + k)] = best[:, k * ROWS:(k + 1) * ROWS]
    rows = jnp.maximum(rows, rows_in_ref[...])
    line = jnp.max(jnp.transpose(rows, (1, 0)), axis=0, keepdims=True)
    for s in range(NEAR - 1):
        for k, ref in enumerate((mine_ref, theirs_ref)):
            at = 2 * s + k
            ref[s] = jnp.where(valid_ref[at] > 0.5, line[:, at * ROWS:(at + 1) * ROWS], -1.0)


def cost(blocks):
    return pl.CostEstimate(
        flops=2 * LEFT * blocks * ROWS * D, bytes_accessed=2 * (2 * NEAR + blocks) * PACK * D, transcendentals=0
    )


def first_maxima(near, panel):
    inside = pl.BlockSpec(memory_space=pltpu.VMEM)
    blocks = len(panel)
    return pl.pallas_call(
        first_kernel,
        out_shape=(
            jax.ShapeDtypeStruct((2 * X, 1, ROWS), jnp.float32),
            jax.ShapeDtypeStruct((LEFT - 2 * ROWS, 128), jnp.float32),
            jax.ShapeDtypeStruct((LEFT, D), jnp.bfloat16),
            jax.ShapeDtypeStruct((LEFT, 128), jnp.float32),
            jax.ShapeDtypeStruct((2 * (NEAR - 1), 1, ROWS), jnp.float32),
        ),
        in_specs=[inside] * (len(near) + blocks),
        out_specs=(inside,) * 5,
        scratch_shapes=[pltpu.VMEM((blocks * ROWS, D), jnp.bfloat16)],
        compiler_params=pltpu.CompilerParams(vmem_limit_bytes=20 * 1024 * 1024),
        name="first_maxima",
        cost_estimate=cost(blocks),
    )(*panel, *near)


def last_maxima(panel, carried):
    inside = pl.BlockSpec(memory_space=pltpu.VMEM)
    lines = jax.ShapeDtypeStruct((NEAR - 1, 1, ROWS), jnp.float32)
    blocks = 2 * X - FIRST
    return pl.pallas_call(
        last_kernel,
        out_shape=(jax.ShapeDtypeStruct((2 * X, 1, ROWS), jnp.float32), lines, lines),
        in_specs=[inside] * (len(panel) + len(carried)),
        out_specs=(inside,) * 3,
        scratch_shapes=[pltpu.VMEM((blocks * ROWS, D), jnp.bfloat16)],
        compiler_params=pltpu.CompilerParams(vmem_limit_bytes=20 * 1024 * 1024),
        name="last_maxima",
        cost_estimate=cost(blocks),
    )(*panel, *carried)


def shift(value, steps, count):
    pairs = [(i, i + steps) for i in range(count) if 0 <= i + steps < count]
    return lax.ppermute(value, "grp", pairs)


def swap(value, axis):
    return lax.ppermute(value, axis, [(0, 1), (1, 0)])


def turn_x(value, even):
    pairs = [(2 * i, 2 * ((i + even) % X)) for i in range(X)]
    pairs += [(2 * i + 1, 2 * ((i + X - even) % X) + 1) for i in range(X)]
    return lax.ppermute(value, ("x", "core"), pairs)


def per_device(embeddings, labels, order):
    count = lax.axis_size("grp")
    grp = lax.axis_index("grp")
    block, tall = pack(embeddings, labels, order)
    one, far, two = (shift(block, steps, count) for steps in MOVES)
    ahead, behind = turn_x(block, 1), turn_x(block, -1)
    across = turn_x(ahead, 1)
    sib = swap(block, "core")
    flipped = gate(swap(tall, "zh"), ahead)
    flip_ahead = turn_x(flipped, 1)
    flip_behind = turn_x(gate(flipped, behind), -1)
    flip_across = turn_x(flip_ahead, 1)
    mine = (block, stack((one, far)), two)
    theirs = [swap(value, "core") for value in mine]
    carried = first_maxima((*mine, *theirs), [block, flipped, ahead, flip_ahead, behind, flip_behind])
    cols, rows, rows_sib = last_maxima([across, flip_across], carried)
    best = jnp.max(lax.all_to_all(cols, ("zh", "x"), 0, 0, tiled=True), axis=0)
    mine = jnp.maximum(rows, swap(rows_sib, "core"))
    for i, steps in enumerate(MOVES):
        back = shift(mine[i], -steps, count)
        source = grp + steps
        best = jnp.maximum(best, jnp.where((source >= 0) & (source < count), back, -1.0))
    return best.reshape(ROWS)


def solution(mesh):
    axes = ("grp", "zh", "x", "core")
    fine = Mesh(mesh.devices.reshape(mesh.shape["grp"], 2, X, 2), axes)
    return jax.shard_map(
        per_device,
        mesh=fine,
        in_specs=(P(axes, None), P(axes), P(axes)),
        out_specs=P(axes),
        check_vma=False,
    )
```
